128 devices in a mesh: shot: 16 (over y, x), head: 8 (over z, core).
Axes of the slice: x: 4, y: 4, z: 4, core: 2. Of those that a mesh axis runs over, the one named last changes fastest.
Arguments:
- projected: bfloat16 [32, 384, 3, 3072], P('shot', None, None, 'head'), may hold values from -12 to 12
- pairs: int32 [64, 2], replicated, may hold values from 0 to 31, as said below
- w_out: bfloat16 [3072, 3072], P('head'), may hold values from -0.15625 to 0.15625
Outputs:
- mixed: bfloat16 [32, 384, 3072], P('shot', None, 'head')
The draws below stay inside these ranges and needn't reach their ends.
Inputs may be any that keep to these rules, and one draw needn't show every extreme that they name: `pairs`: the 8 shots named in one owner's rows lie on pairwise different indices of shot, shot s lying on index s // 2.
All inputs are finite; a program needn't handle non-finite values.
Results may differ from the reference program's by a relative error of at most 0.011.
Values may be sent and summed in bfloat16 or wider, within the bound.
No kernel may reach another device: no remote copies, remote signals or barrier semaphores. Data moves between devices by JAX's collectives and lax.ppermute only.
A program may use at most 128 MiB of HBM per device.

```python
import jax
import jax.numpy as jnp
from jax import lax

D = 3072
HEADS = 24
HEAD_DIM = 128
SEQ = 384
SHOT_DEV = 2
SHOTS = 32
PAIR_DEV = 4
PAIRS = 64


def draw_projected(key, part):
    key = jax.random.fold_in(key, 11)
    key_a = jax.random.fold_in(key, 0)
    width = HEADS * HEAD_DIM
    full_shape = (SHOTS, SEQ, 3, width)
    drawn_values = jnp.clip(jax.random.normal(key_a, full_shape), -6.0, 6.0)
    return drawn_values.astype(jnp.bfloat16)


def draw_pairs(key, part):
    key = jax.random.fold_in(key, 7)
    devices = SHOTS // SHOT_DEV
    picked_count = 2 * PAIR_DEV

    def owner_pairs(owner_index):
        owner_key = jax.random.fold_in(key, owner_index)
        key_a, key_b, key_c = jax.random.split(owner_key, 3)
        others = (owner_index + 1 + jax.random.permutation(key_a, devices - 1)) % devices
        chosen = jnp.concatenate([owner_index[None], others[:picked_count - 1]])
        chosen = chosen[jax.random.permutation(key_b, picked_count)]
        slot_bits = jax.random.randint(key_c, (picked_count,), 0, SHOT_DEV)
        forced = jnp.where(owner_index == 0, 0, SHOT_DEV - 1)
        pinned = (chosen == owner_index) & ((owner_index == 0) | (owner_index == devices - 1))
        slot_bits = jnp.where(pinned, forced, slot_bits)
        return (chosen * SHOT_DEV + slot_bits).reshape(PAIR_DEV, 2)
    owner_list = jnp.arange(devices, dtype=jnp.int32)
    every_pair = jax.vmap(owner_pairs)(owner_list)
    return every_pair.reshape(PAIRS, 2).astype(jnp.int32)


def spiked(values, stream_key, source, target, shards_of, factor):
    def block_of(position):
        return (jnp.arange(values.shape[position]) // (values.shape[position] // shards_of)).reshape((-1,) + (1,) * (values.ndim - 1 - position))

    one_side = jax.random.permutation(stream_key, shards_of)[block_of(target)]
    other_side = (block_of(target) + shards_of // 2) % shards_of
    return jnp.where((block_of(source) == one_side) | (block_of(source) == other_side), factor * values, values)


def steps_of(own_key, extent, cuts, low, largest):
    factor_of, own = 1.0, jax.random.fold_in(own_key, 6)
    for axis_at, blocks in cuts:
        draws = jnp.exp(jax.random.uniform(jax.random.fold_in(own, axis_at), (blocks,), jnp.float32, low / len(cuts), largest / len(cuts)))
        factor_of = factor_of * jnp.repeat(draws, extent[axis_at] // blocks).reshape([-1 if axis == axis_at else 1 for axis in range(len(extent))])
    return factor_of


def bell_draw_with(own_key, dims, spread, limit, shards, heavy, held_as=jnp.bfloat16):
    result = spread * jax.random.normal(own_key, dims, jnp.float32)
    if shards:
        result = result * steps_of(own_key, dims, shards, -0.22, 0.18)
    return jnp.clip(spiked(result, jax.random.fold_in(own_key, 3), *heavy), -limit, limit).astype(held_as)


def setup_inputs(seed: int = 0) -> dict:
    key_list = jax.random.split(jax.random.key(seed), 4)
    return {
        "projected": draw_projected(jax.random.fold_in(key_list[3], 71), 0),
        "pairs": draw_pairs(jax.random.fold_in(key_list[3], 71), 0),
        "w_out": bell_draw_with(key_list[2], (HEADS * HEAD_DIM, D), (HEADS * HEAD_DIM) ** -0.5, 0.15625, ((0, 8),), (0, 1, 8, 2.0)),
    }


def attend_block(query_rows, key_rows, value_rows):
    token_count = query_rows.shape[0]
    head_count = query_rows.shape[1] // HEAD_DIM
    query_heads = query_rows.reshape(token_count, head_count, HEAD_DIM).astype(jnp.float32)
    key_heads = key_rows.reshape(key_rows.shape[0], head_count, HEAD_DIM).astype(jnp.float32)
    value_heads = value_rows.reshape(value_rows.shape[0], head_count, HEAD_DIM).astype(jnp.float32)
    scores = jnp.einsum("qhd,khd->hqk", query_heads, key_heads) * (HEAD_DIM ** -0.5)
    row_peak = jnp.max(scores, axis=-1)
    exponent = jnp.exp(scores - row_peak[:, :, None])
    row_total = jnp.sum(exponent, axis=-1)
    weights = lax.optimization_barrier(exponent.astype(jnp.bfloat16)).astype(jnp.float32)
    combined = jnp.einsum("hqk,khd->qhd", weights, value_heads)
    normed = (combined / jnp.transpose(row_total)[:, :, None]).astype(jnp.bfloat16)
    return normed.reshape(token_count, -1), row_peak + jnp.log(row_total)


def reference(projected, pairs, w_out):
    every_shot = jnp.arange(SHOTS, dtype=jnp.int32)
    query_ids = jnp.concatenate([pairs[:, 0], pairs[:, 1], every_shot]).astype(jnp.int32)
    key_ids = jnp.concatenate([pairs[:, 1], pairs[:, 0], every_shot]).astype(jnp.int32)

    def one_block(ids):
        query_shot, key_shot = ids
        return attend_block(projected[query_shot, :, 0], projected[key_shot, :, 1], projected[key_shot, :, 2])

    normed_all, lse_all = lax.map(one_block, (query_ids, key_ids))
    peak = jax.ops.segment_max(lse_all, query_ids, num_segments=SHOTS)
    weights = jnp.exp(lse_all - peak[query_ids])
    totals = jax.ops.segment_sum(weights, query_ids, num_segments=SHOTS)

    def accumulate(running, entry):
        normed, weight, target = entry
        contribution = normed.reshape(SEQ, HEADS, HEAD_DIM).astype(jnp.float32) * jnp.transpose(weight)[:, :, None]
        return running.at[target].add(contribution), None

    start_value = jnp.zeros((SHOTS, SEQ, HEADS, HEAD_DIM), jnp.float32)
    summed, _ = lax.scan(accumulate, start_value, (normed_all, weights, query_ids))
    attended = (summed / jnp.transpose(totals, (0, 2, 1))[:, :, :, None]).astype(jnp.bfloat16)
    attended = attended.reshape(SHOTS * SEQ, HEADS * HEAD_DIM)
    mixed = jnp.dot(attended, w_out, preferred_element_type=jnp.float32).astype(jnp.bfloat16)
    return mixed.reshape(SHOTS, SEQ, D)
```

```python
import functools

import jax
import jax.numpy as jnp
import numpy as np
from jax import lax
from jax.experimental import pallas as pl
from jax.experimental.pallas import tpu as pltpu
from jax.sharding import PartitionSpec as P

HEAD_DIM = 128
ONES = 16
SCALE = float(np.log2(np.e) / np.sqrt(HEAD_DIM))
VMEM_LIMIT = 48 * 1024 * 1024


def prep_kernel(local_ref, query_ref, first_ref, second_ref):
    for shot, item_ref in enumerate((first_ref, second_ref)):
        query_ref[shot] = local_ref[shot, 0].T
        item_ref[0] = local_ref[shot, 1]
        item_ref[1] = local_ref[shot, 2].T


def prepare(local):
    shots, _, tokens, width = local.shape
    item = jax.ShapeDtypeStruct((2, width, tokens), local.dtype)
    return pl.pallas_call(
        prep_kernel,
        out_shape=[jax.ShapeDtypeStruct((shots, width, tokens), local.dtype), item, item],
        compiler_params=pltpu.CompilerParams(vmem_limit_bytes=VMEM_LIMIT),
        name="prepare",
    )(local)


def attend_kernel(places, arrays, first, last, count_ref, query_ref, *refs):
    item_refs, refs = refs[:arrays], refs[arrays:]
    if not first:
        old_acc_ref, old_top_ref, *refs = refs
    if last:
        out_ref, acc_ref, top_ref, key_buf, value_buf, sems = refs
    else:
        acc_ref, top_ref, key_buf, value_buf, sems = refs
    shots = query_ref.shape[0]
    heads = query_ref.shape[1] // HEAD_DIM
    tokens = query_ref.shape[2]

    def copies(slot):
        array, at = places[slot]
        source = item_refs[array] if at is None else item_refs[array].at[at]
        found = [pltpu.make_async_copy(source.at[0], key_buf.at[slot], sems.at[slot])]
        for head in range(heads):
            found.append(
                pltpu.make_async_copy(
                    source.at[1, pl.ds(head * HEAD_DIM, HEAD_DIM)],
                    value_buf.at[slot, head, pl.ds(0, HEAD_DIM)],
                    sems.at[slot],
                )
            )
        return found

    def used(slot):
        return count_ref[slot, 0] + count_ref[slot, 1] > 0

    for slot in range(len(places)):
        @pl.when(used(slot))
        def _():
            for copy in copies(slot):
                copy.start()

    for slot in range(len(places)):
        for head in range(heads):
            value_buf[slot, head, HEAD_DIM:] = jnp.ones((ONES, tokens), jnp.bfloat16)
    if first:
        acc_ref[...] = jnp.zeros_like(acc_ref)
        top_ref[...] = jnp.full_like(top_ref, -1e30)
    else:
        acc_ref[...] = old_acc_ref[...]
        top_ref[...] = old_top_ref[...]

    for slot in range(len(places)):
        @pl.when(used(slot))
        def _():
            for copy in copies(slot):
                copy.wait()

    def step(index, carry):
        slot, shot = index // shots, index % shots
        times = count_ref[slot, shot]

        @pl.when(times > 0)
        def _():
            for head in range(heads):
                rows = pl.ds(head * HEAD_DIM, HEAD_DIM)
                scores = jnp.dot(
                    key_buf[slot, :, rows], query_ref[shot, rows, :],
                    preferred_element_type=jnp.float32,
                )
                old_top = top_ref[shot, head, 0:1, :]
                new_top = jnp.maximum(old_top, jnp.max(scores, axis=0, keepdims=True))
                expo = jnp.exp2(scores * SCALE - new_top * SCALE).astype(jnp.bfloat16)
                part = jnp.dot(value_buf[slot, head], expo, preferred_element_type=jnp.float32)
                fade = jnp.exp2((old_top - new_top) * SCALE)
                acc_ref[shot, head] = (
                    acc_ref[shot, head] * fade
                    + part[: HEAD_DIM + 8] * times.astype(jnp.float32)
                )
                top_ref[shot, head] = jnp.broadcast_to(new_top, (8, tokens))

        return carry

    lax.fori_loop(0, len(places) * shots, step, 0)
    if last:
        for shot in range(shots):
            for head in range(heads):
                total = acc_ref[shot, head, HEAD_DIM : HEAD_DIM + 1, :]
                value = acc_ref[shot, head, :HEAD_DIM, :] / total
                out_ref[pl.ds(shot * tokens, tokens), pl.ds(head * HEAD_DIM, HEAD_DIM)] = (
                    value.T.astype(out_ref.dtype)
                )


def attend(count, query, arrays, places, state, last):
    shots, width, tokens = query.shape
    heads = width // HEAD_DIM
    acc = jax.ShapeDtypeStruct((shots, heads, HEAD_DIM + 8, tokens), jnp.float32)
    top = jax.ShapeDtypeStruct((shots, heads, 8, tokens), jnp.float32)
    first = state is None
    vmem = pl.BlockSpec(memory_space=pltpu.VMEM)
    slots = len(places)
    scratch = [
        pltpu.VMEM((slots, tokens, width), jnp.bfloat16),
        pltpu.VMEM((slots, heads, HEAD_DIM + ONES, tokens), jnp.bfloat16),
        pltpu.SemaphoreType.DMA((slots,)),
    ]
    if last:
        out_shape = jax.ShapeDtypeStruct((shots * tokens, width), jnp.bfloat16)
        out_specs = vmem
        scratch = [pltpu.VMEM(acc.shape, acc.dtype), pltpu.VMEM(top.shape, top.dtype)] + scratch
    else:
        out_shape, out_specs = [acc, top], [vmem, vmem]
    blocks = 4 if slots <= 4 else 10
    return pl.pallas_call(
        functools.partial(attend_kernel, places, len(arrays), first, last),
        out_shape=out_shape,
        in_specs=[pl.BlockSpec(memory_space=pltpu.SMEM), vmem]
        + [pl.BlockSpec(memory_space=pl.ANY)] * len(arrays)
        + [vmem] * (0 if first else 2),
        out_specs=out_specs,
        scratch_shapes=scratch,
        compiler_params=pltpu.CompilerParams(vmem_limit_bytes=VMEM_LIMIT),
        cost_estimate=pl.CostEstimate(
            flops=blocks * heads * 4 * tokens * tokens * HEAD_DIM,
            bytes_accessed=slots * 2 * width * tokens * 2 + 4 * acc.size * 2,
            transcendentals=blocks * heads * tokens * tokens,
        ),
        name="attend",
    )(count, query, *arrays, *(() if first else state))


def ring(size, step, stride):
    return [(i, (i + step * stride) % size) for i in range(size)]


def project(attended, w_out, w_parts):
    head_count = lax.axis_size("head")
    index = lax.axis_index("head")
    moves = (2, head_count - 2, 4)
    near = [lax.ppermute(attended, "head", ring(head_count, 1, m)) for m in moves]
    wide = 2 * (w_out.shape[1] // head_count)
    own = lax.dynamic_slice_in_dim(w_out, (index // 2) * wide, wide, 1)
    total = jnp.dot(attended, own, preferred_element_type=jnp.float32)
    for got, weight in zip(near, w_parts):
        total = total + jnp.dot(got, weight, preferred_element_type=jnp.float32)
    half = wide // 2
    core = index % 2
    keep = lax.dynamic_slice_in_dim(total, core * half, half, 1)
    give = lax.dynamic_slice_in_dim(total, (1 - core) * half, half, 1).astype(jnp.bfloat16)
    swap = [(i, i ^ 1) for i in range(head_count)]
    other = lax.ppermute(give, "head", swap)
    return (keep + other.astype(jnp.float32)).astype(jnp.bfloat16)


def weight_parts(w_out):
    head_count = lax.axis_size("head")
    index = lax.axis_index("head")
    wide = 2 * (w_out.shape[1] // head_count)
    parts = []
    for move in (2, head_count - 2, 4):
        to = (index + move) % head_count
        part = lax.dynamic_slice_in_dim(w_out, (to // 2) * wide, wide, 1)
        parts.append(lax.ppermute(part, "head", ring(head_count, 1, move)))
    return parts


def body(projected, pairs, w_out):
    me = lax.axis_index("shot")
    shots, tokens, _, width = projected.shape
    all_shots = shots * lax.axis_size("shot")
    local = jnp.transpose(projected, (0, 2, 1, 3))
    query, first, second = prepare(local)
    w_parts = weight_parts(w_out)

    own = (me * shots + jnp.arange(shots, dtype=jnp.int32))[None, :, None]
    other = jnp.arange(all_shots, dtype=jnp.int32)[:, None, None]
    left, right = pairs[:, 0][None, None, :], pairs[:, 1][None, None, :]
    counts = jnp.sum(
        ((left == own) & (right == other)).astype(jnp.int32)
        + ((right == own) & (left == other)).astype(jnp.int32),
        axis=2,
    )
    state = attend(jnp.eye(shots, dtype=jnp.int32), query, [first, second],
                   [(0, None), (1, None)], None, False)
    every = lax.all_gather(jnp.stack([first, second]), "shot", axis=0, tiled=True)
    attended = attend(counts, query, [every], [(0, t) for t in range(all_shots)], state, True)
    mixed = project(attended, w_out, w_parts)
    return mixed.reshape(shots, tokens, mixed.shape[1])


def solution(mesh):
    in_specs = (P("shot", None, None, "head"), P(), P("head", None))
    out_specs = P("shot", None, "head")
    return jax.shard_map(body, mesh=mesh, in_specs=in_specs, out_specs=out_specs, check_vma=False)
```

```python
import functools

import jax
import jax.numpy as jnp
import numpy as np
from jax import lax
from jax.experimental import pallas as pl
from jax.experimental.pallas import tpu as pltpu
from jax.sharding import PartitionSpec as P

HEAD_DIM = 128
ONES = 16
SCALE = float(np.log2(np.e) / np.sqrt(HEAD_DIM))
VMEM_LIMIT = 48 * 1024 * 1024
SIDE = 4
GRID = SIDE * SIDE
VARIANTS = 8
LANES = GRID * VARIANTS
WAYS = 4
STEPS = 5
SEND_AT = 32
STEPS_AT = 64


def neighbour(index, way):
    x, y = index % SIDE, index // SIDE
    dx, dy = ((-1, 0), (1, 0), (0, -1), (0, 1))[way]
    return (y + dy) % SIDE * SIDE + (x + dx) % SIDE


def permutation(way):
    return [(neighbour(index, way), index) for index in range(GRID)]


def route_tables():
    lane = np.arange(LANES)
    index, same = lane % GRID, lane[:, None] // GRID == lane[None, :] // GRID

    def ring_hops(a, b):
        return np.minimum((a - b) % SIDE, (b - a) % SIDE)

    hops = ring_hops(index[:, None] % SIDE, index[None, :] % SIDE) + ring_hops(
        index[:, None] // SIDE, index[None, :] // SIDE
    )
    near = np.concatenate([same & (hops == d) for d in range(1, 5)], 1)
    gain = np.concatenate([(same & (hops < d)) * 2.0**d for d in range(1, 5)], 0)
    source = np.concatenate(
        [
            same & (index[:, None] == np.array([neighbour(j, way) for j in index])[None, :])
            for way in range(WAYS)
        ],
        1,
    )
    noise = 3.0 * np.random.RandomState(0).rand(WAYS, 2 * GRID, LANES)
    as_bf16 = [jnp.asarray(np.asarray(a, np.float32), jnp.bfloat16) for a in (near, gain, source, same)]
    return as_bf16 + [jnp.asarray(noise, jnp.float32)]


def schedule_kernel(me_ref, need_ref, near_ref, gain_ref, source_ref, same_ref, noise_ref, out_ref, rows_ref):
    shots = need_ref.shape[0]
    item = lax.broadcasted_iota(jnp.int32, (shots, LANES), 0)
    lane = lax.broadcasted_iota(jnp.int32, (shots, LANES), 1)
    index = lane % GRID
    need = need_ref[...]
    has = (item // 2 == index).astype(jnp.float32)
    rows_ref[...] = jnp.full(rows_ref.shape, -1.0, jnp.float32)
    taken = jnp.zeros((1, LANES), jnp.float32)

    def dot(a, b):
        return jnp.dot(a.astype(jnp.bfloat16), b, preferred_element_type=jnp.float32)

    def open_groups(held):
        missing = jnp.max(need * (1.0 - held), axis=0, keepdims=True)
        return jnp.minimum(dot(jnp.broadcast_to(missing, (16, LANES)), same_ref[...])[0:1], 1.0)

    for step in range(STEPS + 1):
        taken = taken + open_groups(has)
        if step == STEPS:
            break
        offered = dot(has, source_ref[...])
        held = has
        for way in range(WAYS):
            there = offered[:, way * LANES : (way + 1) * LANES]
            if step == 0:
                good = (there > 0.5) & (item % 2 == way // 2)
                picked = jnp.min(jnp.where(good, item, shots), axis=0, keepdims=True)
            else:
                reach = dot(held, near_ref[...])
                rest = need * (1.0 - held)
                far = 1.0 - held
                parts = []
                for d in range(4):
                    at = reach[:, d * LANES : (d + 1) * LANES] > 0.5
                    parts.append(jnp.where(at, rest * far, 0.0))
                    far = jnp.where(at, 0.0, far)
                score = dot(jnp.concatenate(parts, axis=1), gain_ref[...]) + 1.5 * rest
                good = (there > 0.5) & (held < 0.5) & (score > 0.0)
                score = jnp.where(good, score + noise_ref[(way + step) % WAYS], -1.0)
                best = jnp.max(score, axis=0, keepdims=True)
                picked = jnp.min(jnp.where(good & (score == best), item, shots), axis=0, keepdims=True)
            held = jnp.where(item == picked, 1.0, held)
            row = step * WAYS + way
            rows_ref[pl.ds(row, 1), :] = jnp.where(picked == shots, -1, picked).astype(jnp.float32)
        has = held

    first_lane = lax.broadcasted_iota(jnp.int32, (1, LANES), 1)
    rank = taken * LANES + (first_lane // GRID).astype(jnp.float32)
    least = jnp.min(rank, axis=1, keepdims=True)
    base = jnp.min(jnp.where(rank == least, first_lane, LANES), axis=1, keepdims=True)
    me = me_ref[0]
    x, y = me % SIDE, me // SIDE
    rows = rows_ref[...]
    row = lax.broadcasted_iota(jnp.int32, rows.shape, 0)
    column = lax.broadcasted_iota(jnp.int32, rows.shape, 1)
    way = row % WAYS
    target = jnp.where(
        way == 0,
        y * SIDE + (x + 1) % SIDE,
        jnp.where(
            way == 1,
            y * SIDE + (x + SIDE - 1) % SIDE,
            jnp.where(way == 2, (y + 1) % SIDE * SIDE + x, (y + SIDE - 1) % SIDE * SIDE + x),
        ),
    )
    got = jnp.sum(jnp.where(column == base + me, rows, 0.0), axis=1, keepdims=True)
    sent = jnp.sum(jnp.where(column == base + target, rows, 0.0), axis=1, keepdims=True)
    table = jnp.where(column == row, got, 0.0) + jnp.where(column == row + SEND_AT, sent, 0.0)
    table = jnp.sum(table, axis=0, keepdims=True)
    needed = jnp.sum(jnp.where(first_lane == base, taken, 0.0), axis=1, keepdims=True)
    table = jnp.where(first_lane == STEPS_AT, needed, table)
    out_ref[...] = jnp.broadcast_to(table, out_ref.shape).astype(jnp.int32)


def schedule(pairs, me, shots):
    left, right = pairs[:, 0][None, None, :], pairs[:, 1][None, None, :]
    item = jnp.arange(shots, dtype=jnp.int32)[:, None, None]
    index = (jnp.arange(LANES, dtype=jnp.int32) % GRID)[None, :, None]
    need = jnp.any(
        ((left == item) & (right // 2 == index)) | ((right == item) & (left // 2 == index)), axis=2
    ).astype(jnp.float32)
    vmem = pl.BlockSpec(memory_space=pltpu.VMEM)
    return pl.pallas_call(
        schedule_kernel,
        out_shape=jax.ShapeDtypeStruct((8, LANES), jnp.int32),
        in_specs=[pl.BlockSpec(memory_space=pltpu.SMEM)] + [vmem] * 6,
        out_specs=vmem,
        scratch_shapes=[pltpu.VMEM((32, LANES), jnp.float32)],
        compiler_params=pltpu.CompilerParams(vmem_limit_bytes=VMEM_LIMIT),
        cost_estimate=pl.CostEstimate(flops=100_000_000, bytes_accessed=10_000_000, transcendentals=0),
        name="schedule",
    )(me[None], need, *route_tables())


def prep_kernel(local_ref, query_ref, first_ref, second_ref):
    for shot, item_ref in enumerate((first_ref, second_ref)):
        query_ref[shot] = local_ref[shot, 0].T
        item_ref[0] = local_ref[shot, 1]
        item_ref[1] = local_ref[shot, 2].T


def prepare(local):
    shots, _, tokens, width = local.shape
    item = jax.ShapeDtypeStruct((2, width, tokens), local.dtype)
    return pl.pallas_call(
        prep_kernel,
        out_shape=[jax.ShapeDtypeStruct((shots, width, tokens), local.dtype), item, item],
        compiler_params=pltpu.CompilerParams(vmem_limit_bytes=VMEM_LIMIT),
        name="prepare",
    )(local)


def attend_kernel(places, arrays, kind, first, last, table_ref, count_ref, query_ref, *refs):
    item_refs, refs = refs[:arrays], refs[arrays:]
    if not first:
        old_acc_ref, old_top_ref, *refs = refs
    if last:
        out_ref, acc_ref, top_ref, key_buf, value_buf, sems = refs
    else:
        acc_ref, top_ref, key_buf, value_buf, sems = refs
    shots = query_ref.shape[0]
    heads = query_ref.shape[1] // HEAD_DIM
    tokens = query_ref.shape[2]

    def copies(slot):
        array, at = places[slot]
        source = item_refs[array] if at is None else item_refs[array].at[at]
        found = [pltpu.make_async_copy(source.at[0], key_buf.at[slot], sems.at[slot])]
        for head in range(heads):
            found.append(
                pltpu.make_async_copy(
                    source.at[1, pl.ds(head * HEAD_DIM, HEAD_DIM)],
                    value_buf.at[slot, head, pl.ds(0, HEAD_DIM)],
                    sems.at[slot],
                )
            )
        return found

    def times_of(slot, shot):
        if kind == "own":
            return jnp.where(slot == shot, 1, 0)
        if kind == "all":
            return count_ref[slot, shot]
        item = table_ref[0, kind * WAYS + slot]
        return jnp.where(item >= 0, count_ref[jnp.maximum(item, 0), shot], 0)

    def used(slot):
        return sum(times_of(slot, shot) for shot in range(shots)) > 0

    for slot in range(len(places)):
        @pl.when(used(slot))
        def _():
            for copy in copies(slot):
                copy.start()

    for slot in range(len(places)):
        for head in range(heads):
            value_buf[slot, head, HEAD_DIM:] = jnp.ones((ONES, tokens), jnp.bfloat16)
    if first:
        acc_ref[...] = jnp.zeros_like(acc_ref)
        top_ref[...] = jnp.full_like(top_ref, -1e30)
    else:
        acc_ref[...] = old_acc_ref[...]
        top_ref[...] = old_top_ref[...]

    for slot in range(len(places)):
        @pl.when(used(slot))
        def _():
            for copy in copies(slot):
                copy.wait()

    def step(index, carry):
        slot, shot = index // shots, index % shots
        times = times_of(slot, shot)

        @pl.when(times > 0)
        def _():
            for head in range(heads):
                rows = pl.ds(head * HEAD_DIM, HEAD_DIM)
                scores = jnp.dot(
                    key_buf[slot, :, rows], query_ref[shot, rows, :],
                    preferred_element_type=jnp.float32,
                )
                old_top = top_ref[shot, head, 0:1, :]
                new_top = jnp.maximum(old_top, jnp.max(scores, axis=0, keepdims=True))
                expo = jnp.exp2(scores * SCALE - new_top * SCALE).astype(jnp.bfloat16)
                part = jnp.dot(value_buf[slot, head], expo, preferred_element_type=jnp.float32)
                fade = jnp.exp2((old_top - new_top) * SCALE)
                acc_ref[shot, head] = (
                    acc_ref[shot, head] * fade
                    + part[: HEAD_DIM + 8] * times.astype(jnp.float32)
                )
                top_ref[shot, head] = jnp.broadcast_to(new_top, (8, tokens))

        return carry

    lax.fori_loop(0, len(places) * shots, step, 0)
    if last:
        for shot in range(shots):
            for head in range(heads):
                total = acc_ref[shot, head, HEAD_DIM : HEAD_DIM + 1, :]
                value = acc_ref[shot, head, :HEAD_DIM, :] / total
                out_ref[pl.ds(shot * tokens, tokens), pl.ds(head * HEAD_DIM, HEAD_DIM)] = (
                    value.T.astype(out_ref.dtype)
                )


def attend(kind, table, count, query, arrays, places, state, last):
    shots, width, tokens = query.shape
    heads = width // HEAD_DIM
    acc = jax.ShapeDtypeStruct((shots, heads, HEAD_DIM + 8, tokens), jnp.float32)
    top = jax.ShapeDtypeStruct((shots, heads, 8, tokens), jnp.float32)
    first = state is None
    vmem = pl.BlockSpec(memory_space=pltpu.VMEM)
    slots = len(places)
    scratch = [
        pltpu.VMEM((slots, tokens, width), jnp.bfloat16),
        pltpu.VMEM((slots, heads, HEAD_DIM + ONES, tokens), jnp.bfloat16),
        pltpu.SemaphoreType.DMA((slots,)),
    ]
    if last:
        out_shape = jax.ShapeDtypeStruct((shots * tokens, width), jnp.bfloat16)
        out_specs = vmem
        scratch = [pltpu.VMEM(acc.shape, acc.dtype), pltpu.VMEM(top.shape, top.dtype)] + scratch
    else:
        out_shape, out_specs = [acc, top], [vmem, vmem]
    blocks = 2 if slots <= 4 else 10
    return pl.pallas_call(
        functools.partial(attend_kernel, places, len(arrays), kind, first, last),
        out_shape=out_shape,
        in_specs=[pl.BlockSpec(memory_space=pltpu.SMEM)] * 2
        + [vmem]
        + [pl.BlockSpec(memory_space=pl.ANY)] * len(arrays)
        + [vmem] * (0 if first else 2),
        out_specs=out_specs,
        scratch_shapes=scratch,
        compiler_params=pltpu.CompilerParams(vmem_limit_bytes=VMEM_LIMIT),
        cost_estimate=pl.CostEstimate(
            flops=blocks * heads * 4 * tokens * tokens * HEAD_DIM,
            bytes_accessed=slots * 2 * width * tokens * 2 + 4 * acc.size * 2,
            transcendentals=blocks * heads * tokens * tokens,
        ),
        name="attend",
    )(table, count, query, *arrays, *(() if first else state))


def pick_kernel(step, held, table_ref, *refs):
    item_refs, out_refs, sems = refs[:held], refs[-1 - WAYS : -1], refs[-1]
    shots = 2
    me = lax.axis_index("shot")

    def copy(slot, way):
        return pltpu.make_async_copy(item_refs[slot], out_refs[way], sems.at[way])

    wanted = [table_ref[0, SEND_AT + step * WAYS + way] for way in range(WAYS)]
    for slot in range(held):
        item = me * shots + slot if slot < shots else table_ref[0, slot - shots]
        for way in range(WAYS):
            @pl.when((wanted[way] >= 0) & (wanted[way] == item))
            def _():
                copy(slot, way).start()
    for way in range(WAYS):
        @pl.when(wanted[way] >= 0)
        def _():
            copy(0, way).wait()


def pick(step, table, items, after):
    one = jax.ShapeDtypeStruct(items[0].shape, items[0].dtype)
    return pl.pallas_call(
        functools.partial(pick_kernel, step, len(items)),
        out_shape=[one] * WAYS,
        in_specs=[pl.BlockSpec(memory_space=pltpu.SMEM)]
        + [pl.BlockSpec(memory_space=pl.ANY)] * (len(items) + len(after)),
        out_specs=[pl.BlockSpec(memory_space=pltpu.VMEM)] * WAYS,
        scratch_shapes=[pltpu.SemaphoreType.DMA((WAYS,))],
        compiler_params=pltpu.CompilerParams(vmem_limit_bytes=VMEM_LIMIT),
        cost_estimate=pl.CostEstimate(
            flops=0, bytes_accessed=2 * WAYS * one.size * 2, transcendentals=0
        ),
        name="pick",
    )(table, *items, *after)


def ring(size, step, stride):
    return [(i, (i + step * stride) % size) for i in range(size)]


def project(attended, w_out, w_parts):
    head_count = lax.axis_size("head")
    index = lax.axis_index("head")
    up, down = ring(head_count, 1, 2), ring(head_count, 1, head_count - 2)
    from_below = lax.ppermute(attended, "head", up)
    from_above = lax.ppermute(attended, "head", down)
    rows = attended.shape[0] // 2
    opposite = jnp.concatenate(
        [
            lax.ppermute(from_below[:rows], "head", up),
            lax.ppermute(from_above[rows:], "head", down),
        ]
    )
    near = [from_below, from_above, opposite]
    wide = 2 * (w_out.shape[1] // head_count)
    own = lax.dynamic_slice_in_dim(w_out, (index // 2) * wide, wide, 1)
    total = jnp.dot(attended, own, preferred_element_type=jnp.float32)
    for got, weight in zip(near, w_parts):
        total = total + jnp.dot(got, weight, preferred_element_type=jnp.float32)
    half = wide // 2
    core = index % 2
    keep = lax.dynamic_slice_in_dim(total, core * half, half, 1)
    give = lax.dynamic_slice_in_dim(total, (1 - core) * half, half, 1).astype(jnp.bfloat16)
    swap = [(i, i ^ 1) for i in range(head_count)]
    other = lax.ppermute(give, "head", swap)
    return (keep + other.astype(jnp.float32)).astype(jnp.bfloat16)


def weight_parts(w_out):
    head_count = lax.axis_size("head")
    index = lax.axis_index("head")
    wide = 2 * (w_out.shape[1] // head_count)
    parts = []
    for move in (2, head_count - 2, 4):
        to = (index + move) % head_count
        part = lax.dynamic_slice_in_dim(w_out, (to // 2) * wide, wide, 1)
        parts.append(lax.ppermute(part, "head", ring(head_count, 1, move)))
    return parts


def body(projected, pairs, w_out):
    me = lax.axis_index("shot")
    shots, tokens, _, width = projected.shape
    all_shots = shots * lax.axis_size("shot")
    local = jnp.transpose(projected, (0, 2, 1, 3))
    query, first, second = prepare(local)
    w_parts = weight_parts(w_out)

    own = (me * shots + jnp.arange(shots, dtype=jnp.int32))[None, :, None]
    other = jnp.arange(all_shots, dtype=jnp.int32)[:, None, None]
    left, right = pairs[:, 0][None, None, :], pairs[:, 1][None, None, :]
    counts = jnp.sum(
        ((left == own) & (right == other)).astype(jnp.int32)
        + ((right == own) & (left == other)).astype(jnp.int32),
        axis=2,
    )
    table = schedule(pairs, me, all_shots)
    held = [first, second]
    arrived = []
    for step in range(STEPS):
        if step == 0:
            outs = (first, first, second, second)
        else:
            outs = pick(step, table, held, [state[1]] + (w_parts if step == 2 else []))
        got = [lax.ppermute(out, "shot", permutation(way)) for way, out in enumerate(outs)]
        if step == 0:
            own_state = state = attend(
                "own", table, counts, query, held, [(0, None), (1, None)], None, False
            )
        else:
            state = attend(step - 1, table, counts, query, arrived, each, state, False)
        each = [(way, None) for way in range(WAYS)]
        arrived = got
        held = held + got

    def rest():
        every = lax.all_gather(jnp.stack([first, second]), "shot", axis=0, tiled=True)
        places = [(0, at) for at in range(all_shots)]
        return attend("all", table, counts, query, [every], places, own_state, True)

    def done():
        return attend(STEPS - 1, table, counts, query, arrived, each, state, True)

    attended = lax.cond(table[0, STEPS_AT] > STEPS, rest, done)
    mixed = project(attended, w_out, w_parts)
    return mixed.reshape(shots, tokens, mixed.shape[1])


def solution(mesh):
    in_specs = (P("shot", None, None, "head"), P(), P("head", None))
    out_specs = P("shot", None, "head")
    return jax.shard_map(body, mesh=mesh, in_specs=in_specs, out_specs=out_specs, check_vma=False)
```

```python
import functools

import jax
import jax.numpy as jnp
import numpy as np
from jax import lax
from jax.experimental import pallas as pl
from jax.experimental.pallas import tpu as pltpu
from jax.sharding import PartitionSpec as P

HEAD_DIM = 128
ONES = 16
SCALE = float(np.log2(np.e) / np.sqrt(HEAD_DIM))
VMEM_LIMIT = 16 * 1024 * 1024
SIDE = 4
GRID = SIDE * SIDE
VARIANTS = 8
LANES = GRID * VARIANTS
WAYS = 4
STEPS = 5
SEND_AT = 32
STEPS_AT = 64


def neighbour(index, way):
    x, y = index % SIDE, index // SIDE
    dx, dy = ((-1, 0), (1, 0), (0, -1), (0, 1))[way]
    return (y + dy) % SIDE * SIDE + (x + dx) % SIDE


def permutation(way):
    return [(neighbour(index, way), index) for index in range(GRID)]


def route_tables():
    lane = np.arange(LANES)
    index, same = lane % GRID, lane[:, None] // GRID == lane[None, :] // GRID

    def ring_hops(a, b):
        return np.minimum((a - b) % SIDE, (b - a) % SIDE)

    hops = ring_hops(index[:, None] % SIDE, index[None, :] % SIDE) + ring_hops(
        index[:, None] // SIDE, index[None, :] // SIDE
    )
    near = np.concatenate([same & (hops == d) for d in range(1, 5)], 1)
    gain = np.concatenate([(same & (hops < d)) * 2.0**d for d in range(1, 5)], 0)
    source = np.concatenate(
        [
            same & (index[:, None] == np.array([neighbour(j, way) for j in index])[None, :])
            for way in range(WAYS)
        ],
        1,
    )
    noise = 3.0 * np.random.RandomState(0).rand(WAYS, 2 * GRID, LANES)
    as_bf16 = [jnp.asarray(np.asarray(a, np.float32), jnp.bfloat16) for a in (near, gain, source, same)]
    return as_bf16 + [jnp.asarray(noise, jnp.float32)]


def schedule_kernel(me_ref, need_ref, near_ref, gain_ref, source_ref, same_ref, noise_ref, out_ref, rows_ref):
    shots = need_ref.shape[0]
    item = lax.broadcasted_iota(jnp.int32, (shots, LANES), 0)
    lane = lax.broadcasted_iota(jnp.int32, (shots, LANES), 1)
    index = lane % GRID
    need = need_ref[...]
    has = (item // 2 == index).astype(jnp.float32)
    rows_ref[...] = jnp.full(rows_ref.shape, -1.0, jnp.float32)
    taken = jnp.zeros((1, LANES), jnp.float32)

    def dot(a, b):
        return jnp.dot(a.astype(jnp.bfloat16), b, preferred_element_type=jnp.float32)

    def open_groups(held):
        missing = jnp.max(need * (1.0 - held), axis=0, keepdims=True)
        return jnp.minimum(dot(jnp.broadcast_to(missing, (16, LANES)), same_ref[...])[0:1], 1.0)

    for step in range(STEPS + 1):
        taken = taken + open_groups(has)
        if step == STEPS:
            break
        offered = dot(has, source_ref[...])
        held = has
        for way in range(WAYS):
            there = offered[:, way * LANES : (way + 1) * LANES]
            if step == 0:
                good = (there > 0.5) & (item % 2 == way // 2)
                picked = jnp.min(jnp.where(good, item, shots), axis=0, keepdims=True)
            else:
                reach = dot(held, near_ref[...])
                rest = need * (1.0 - held)
                far = 1.0 - held
                parts = []
                for d in range(4):
                    at = reach[:, d * LANES : (d + 1) * LANES] > 0.5
                    parts.append(jnp.where(at, rest * far, 0.0))
                    far = jnp.where(at, 0.0, far)
                score = dot(jnp.concatenate(parts, axis=1), gain_ref[...]) + 1.5 * rest
                good = (there > 0.5) & (held < 0.5) & (score > 0.0)
                score = jnp.where(good, score + noise_ref[(way + step) % WAYS], -1.0)
                best = jnp.max(score, axis=0, keepdims=True)
                picked = jnp.min(jnp.where(good & (score == best), item, shots), axis=0, keepdims=True)
            held = jnp.where(item == picked, 1.0, held)
            row = step * WAYS + way
            rows_ref[pl.ds(row, 1), :] = jnp.where(picked == shots, -1, picked).astype(jnp.float32)
        has = held

    first_lane = lax.broadcasted_iota(jnp.int32, (1, LANES), 1)
    rank = taken * LANES + (first_lane // GRID).astype(jnp.float32)
    least = jnp.min(rank, axis=1, keepdims=True)
    base = jnp.min(jnp.where(rank == least, first_lane, LANES), axis=1, keepdims=True)
    me = me_ref[0]
    x, y = me % SIDE, me // SIDE
    rows = rows_ref[...]
    row = lax.broadcasted_iota(jnp.int32, rows.shape, 0)
    column = lax.broadcasted_iota(jnp.int32, rows.shape, 1)
    way = row % WAYS
    target = jnp.where(
        way == 0,
        y * SIDE + (x + 1) % SIDE,
        jnp.where(
            way == 1,
            y * SIDE + (x + SIDE - 1) % SIDE,
            jnp.where(way == 2, (y + 1) % SIDE * SIDE + x, (y + SIDE - 1) % SIDE * SIDE + x),
        ),
    )
    got = jnp.sum(jnp.where(column == base + me, rows, 0.0), axis=1, keepdims=True)
    sent = jnp.sum(jnp.where(column == base + target, rows, 0.0), axis=1, keepdims=True)
    table = jnp.where(column == row, got, 0.0) + jnp.where(column == row + SEND_AT, sent, 0.0)
    table = jnp.sum(table, axis=0, keepdims=True)
    needed = jnp.sum(jnp.where(first_lane == base, taken, 0.0), axis=1, keepdims=True)
    table = jnp.where(first_lane == STEPS_AT, needed, table)
    out_ref[...] = jnp.broadcast_to(table, out_ref.shape).astype(jnp.int32)


def schedule(pairs, me, shots):
    left, right = pairs[:, 0][None, None, :], pairs[:, 1][None, None, :]
    item = jnp.arange(shots, dtype=jnp.int32)[:, None, None]
    index = (jnp.arange(LANES, dtype=jnp.int32) % GRID)[None, :, None]
    need = jnp.any(
        ((left == item) & (right // 2 == index)) | ((right == item) & (left // 2 == index)), axis=2
    ).astype(jnp.float32)
    vmem = pl.BlockSpec(memory_space=pltpu.VMEM)
    return pl.pallas_call(
        schedule_kernel,
        out_shape=jax.ShapeDtypeStruct((8, LANES), jnp.int32),
        in_specs=[pl.BlockSpec(memory_space=pltpu.SMEM)] + [vmem] * 6,
        out_specs=vmem,
        scratch_shapes=[pltpu.VMEM((32, LANES), jnp.float32)],
        compiler_params=pltpu.CompilerParams(vmem_limit_bytes=VMEM_LIMIT),
        cost_estimate=pl.CostEstimate(flops=100_000_000, bytes_accessed=10_000_000, transcendentals=0),
        name="schedule",
    )(me[None], need, *route_tables())


def prep_kernel(local_ref, query_ref, first_ref, second_ref):
    for shot, item_ref in enumerate((first_ref, second_ref)):
        query_ref[shot] = local_ref[shot, 0].T
        item_ref[0] = local_ref[shot, 1]
        item_ref[1] = local_ref[shot, 2].T


def prepare(local):
    shots, _, tokens, width = local.shape
    item = jax.ShapeDtypeStruct((2, width, tokens), local.dtype)
    return pl.pallas_call(
        prep_kernel,
        out_shape=[jax.ShapeDtypeStruct((shots, width, tokens), local.dtype), item, item],
        compiler_params=pltpu.CompilerParams(vmem_limit_bytes=VMEM_LIMIT),
        name="prepare",
    )(local)


def attend_kernel(places, arrays, kind, first, last, table_ref, count_ref, query_ref, *refs):
    item_refs, refs = refs[:arrays], refs[arrays:]
    if not first:
        old_acc_ref, old_top_ref, *refs = refs
    if last:
        *out_refs, acc_ref, top_ref, key_buf, value_buf, sems = refs
    else:
        acc_ref, top_ref, key_buf, value_buf, sems = refs
    shots = query_ref.shape[0]
    heads = query_ref.shape[1] // HEAD_DIM
    tokens = query_ref.shape[2]

    def copies(slot):
        array, at = places[slot]
        source = item_refs[array] if at is None else item_refs[array].at[at]
        found = [pltpu.make_async_copy(source.at[0], key_buf.at[slot], sems.at[slot])]
        for head in range(heads):
            found.append(
                pltpu.make_async_copy(
                    source.at[1, pl.ds(head * HEAD_DIM, HEAD_DIM)],
                    value_buf.at[slot, head, pl.ds(0, HEAD_DIM)],
                    sems.at[slot],
                )
            )
        return found

    def times_of(slot, shot):
        if kind == "own":
            return jnp.where(slot == shot, 1, 0)
        item = table_ref[0, kind * WAYS + slot]
        return jnp.where(item >= 0, count_ref[jnp.maximum(item, 0), shot], 0)

    def used(slot):
        return sum(times_of(slot, shot) for shot in range(shots)) > 0

    for slot in range(len(places)):
        @pl.when(used(slot))
        def _():
            for copy in copies(slot):
                copy.start()

    for slot in range(len(places)):
        for head in range(heads):
            value_buf[slot, head, HEAD_DIM:] = jnp.ones((ONES, tokens), jnp.bfloat16)
    if first:
        acc_ref[...] = jnp.zeros_like(acc_ref)
        top_ref[...] = jnp.full_like(top_ref, -1e30)
    else:
        acc_ref[...] = old_acc_ref[...]
        top_ref[...] = old_top_ref[...]

    for slot in range(len(places)):
        @pl.when(used(slot))
        def _():
            for copy in copies(slot):
                copy.wait()

    def step(index, carry):
        slot, shot = index // shots, index % shots
        times = times_of(slot, shot)

        @pl.when(times > 0)
        def _():
            for head in range(heads):
                rows = pl.ds(head * HEAD_DIM, HEAD_DIM)
                scores = jnp.dot(
                    key_buf[slot, :, rows], query_ref[shot, rows, :],
                    preferred_element_type=jnp.float32,
                )
                old_top = top_ref[shot, head, 0:1, :]
                new_top = jnp.maximum(old_top, jnp.max(scores, axis=0, keepdims=True))
                expo = jnp.exp2(scores * SCALE - new_top * SCALE).astype(jnp.bfloat16)
                part = jnp.dot(value_buf[slot, head], expo, preferred_element_type=jnp.float32)
                fade = jnp.exp2((old_top - new_top) * SCALE)
                acc_ref[shot, head] = (
                    acc_ref[shot, head] * fade
                    + part[: HEAD_DIM + 8] * times.astype(jnp.float32)
                )
                top_ref[shot, head] = jnp.broadcast_to(new_top, (8, tokens))

        return carry

    lax.fori_loop(0, len(places) * shots, step, 0)
    if last:
        for shot in range(shots):
            for head in range(heads):
                total = acc_ref[shot, head, HEAD_DIM : HEAD_DIM + 1, :]
                value = acc_ref[shot, head, :HEAD_DIM, :] / total
                out_refs[shot][:, pl.ds(head * HEAD_DIM, HEAD_DIM)] = value.T.astype(jnp.bfloat16)


def attend(kind, table, count, query, arrays, places, state, last):
    shots, width, tokens = query.shape
    heads = width // HEAD_DIM
    acc = jax.ShapeDtypeStruct((shots, heads, HEAD_DIM + 8, tokens), jnp.float32)
    top = jax.ShapeDtypeStruct((shots, heads, 8, tokens), jnp.float32)
    first = state is None
    vmem = pl.BlockSpec(memory_space=pltpu.VMEM)
    slots = len(places)
    scratch = [
        pltpu.VMEM((slots, tokens, width), jnp.bfloat16),
        pltpu.VMEM((slots, heads, HEAD_DIM + ONES, tokens), jnp.bfloat16),
        pltpu.SemaphoreType.DMA((slots,)),
    ]
    if last:
        out_shape = [jax.ShapeDtypeStruct((tokens, width), jnp.bfloat16)] * shots
        out_specs = [vmem] * shots
        scratch = [pltpu.VMEM(acc.shape, acc.dtype), pltpu.VMEM(top.shape, top.dtype)] + scratch
    else:
        out_shape, out_specs = [acc, top], [vmem, vmem]
    blocks = 2
    return pl.pallas_call(
        functools.partial(attend_kernel, places, len(arrays), kind, first, last),
        out_shape=out_shape,
        in_specs=[pl.BlockSpec(memory_space=pltpu.SMEM)] * 2
        + [vmem]
        + [pl.BlockSpec(memory_space=pl.ANY)] * len(arrays)
        + [vmem] * (0 if first else 2),
        out_specs=out_specs,
        scratch_shapes=scratch,
        compiler_params=pltpu.CompilerParams(vmem_limit_bytes=VMEM_LIMIT),
        cost_estimate=pl.CostEstimate(
            flops=blocks * heads * 4 * tokens * tokens * HEAD_DIM,
            bytes_accessed=slots * 2 * width * tokens * 2 + 4 * acc.size * 2,
            transcendentals=blocks * heads * tokens * tokens,
        ),
        name="attend",
    )(table, count, query, *arrays, *(() if first else state))


def pick_kernel(step, held, table_ref, *refs):
    item_refs, out_refs, sems = refs[:held], refs[-1 - WAYS : -1], refs[-1]
    shots = 2
    me = lax.axis_index("shot")

    def copy(slot, way):
        return pltpu.make_async_copy(item_refs[slot], out_refs[way], sems.at[way])

    wanted = [table_ref[0, SEND_AT + step * WAYS + way] for way in range(WAYS)]
    for slot in range(held):
        item = me * shots + slot if slot < shots else table_ref[0, slot - shots]
        for way in range(WAYS):
            @pl.when((wanted[way] >= 0) & (wanted[way] == item))
            def _():
                copy(slot, way).start()
    for way in range(WAYS):
        @pl.when(wanted[way] >= 0)
        def _():
            copy(0, way).wait()


def pick(step, table, items, after):
    one = jax.ShapeDtypeStruct(items[0].shape, items[0].dtype)
    return pl.pallas_call(
        functools.partial(pick_kernel, step, len(items)),
        out_shape=[one] * WAYS,
        in_specs=[pl.BlockSpec(memory_space=pltpu.SMEM)]
        + [pl.BlockSpec(memory_space=pl.ANY)] * (len(items) + len(after)),
        out_specs=[pl.BlockSpec(memory_space=pltpu.VMEM)] * WAYS,
        scratch_shapes=[pltpu.SemaphoreType.DMA((WAYS,))],
        compiler_params=pltpu.CompilerParams(vmem_limit_bytes=VMEM_LIMIT),
        cost_estimate=pl.CostEstimate(
            flops=0, bytes_accessed=2 * WAYS * one.size * 2, transcendentals=0
        ),
        name="pick",
    )(table, *items, *after)


def ring(size, step, stride):
    return [(i, (i + step * stride) % size) for i in range(size)]


def project(attended, w_out, w_parts):
    head_count = lax.axis_size("head")
    index = lax.axis_index("head")
    up, down = ring(head_count, 1, 2), ring(head_count, 1, head_count - 2)
    one, two = attended
    one_up, two_down = lax.ppermute(one, "head", up), lax.ppermute(two, "head", down)
    two_up, one_down = lax.ppermute(two, "head", up), lax.ppermute(one, "head", down)
    one_far, two_far = lax.ppermute(one_up, "head", up), lax.ppermute(two_down, "head", down)
    wide = 2 * (w_out.shape[1] // head_count)
    own = lax.dynamic_slice_in_dim(w_out, (index // 2) * wide, wide, 1)
    weights = [own] + list(w_parts)
    half = wide // 2
    core = index % 2
    swap = [(i, i ^ 1) for i in range(head_count)]
    results = []
    for sources in ((one, one_up, one_down, one_far), (two, two_up, two_down, two_far)):
        total = None
        for rows, weight in zip(sources, weights):
            term = jnp.dot(rows, weight, preferred_element_type=jnp.float32)
            total = term if total is None else total + term
        keep = lax.dynamic_slice_in_dim(total, core * half, half, 1)
        give = lax.dynamic_slice_in_dim(total, (1 - core) * half, half, 1).astype(jnp.bfloat16)
        other = lax.ppermute(give, "head", swap)
        results.append((keep + other.astype(jnp.float32)).astype(jnp.bfloat16))
    return jnp.stack(results)


def weight_parts(w_out):
    head_count = lax.axis_size("head")
    index = lax.axis_index("head")
    wide = 2 * (w_out.shape[1] // head_count)
    parts = []
    for move in (2, head_count - 2, 4):
        to = (index + move) % head_count
        part = lax.dynamic_slice_in_dim(w_out, (to // 2) * wide, wide, 1)
        parts.append(lax.ppermute(part, "head", ring(head_count, 1, move)))
    return parts


def body(projected, pairs, w_out):
    me = lax.axis_index("shot")
    shots, tokens, _, width = projected.shape
    all_shots = shots * lax.axis_size("shot")
    local = jnp.transpose(projected, (0, 2, 1, 3))
    query, first, second = prepare(local)
    w_parts = weight_parts(w_out)

    own = (me * shots + jnp.arange(shots, dtype=jnp.int32))[None, :, None]
    other = jnp.arange(all_shots, dtype=jnp.int32)[:, None, None]
    left, right = pairs[:, 0][None, None, :], pairs[:, 1][None, None, :]
    counts = jnp.sum(
        ((left == own) & (right == other)).astype(jnp.int32)
        + ((right == own) & (left == other)).astype(jnp.int32),
        axis=2,
    )
    table = schedule(pairs, me, all_shots)
    held = [first, second]
    arrived = []
    for step in range(STEPS):
        if step == 0:
            outs = (first, first, second, second)
        else:
            outs = pick(step, table, held, [state[1]] + w_parts[step - 2 : step - 1] * (step > 1))
        got = [lax.ppermute(out, "shot", permutation(way)) for way, out in enumerate(outs)]
        if step == 0:
            own_state = state = attend(
                "own", table, counts, query, held, [(0, None), (1, None)], None, False
            )
        else:
            state = attend(step - 1, table, counts, query, arrived, each, state, False)
        each = [(way, None) for way in range(WAYS)]
        arrived = got
        held = held + got

    attended = attend(STEPS - 1, table, counts, query, arrived, each, state, True)

    def rest(projected, counts, attended):
        query, first, second = prepare(jnp.transpose(projected, (0, 2, 1, 3)))
        size = lax.axis_size("shot")
        both = [(0, None), (1, None)]
        lane = jnp.arange(LANES, dtype=jnp.int32)[None, :] + jnp.zeros((8, 1), jnp.int32)

        def shift(hop, carry):
            items, state = carry
            items = [lax.ppermute(item, "shot", ring(size, 1, 1)) for item in items]
            source = (me + size - 1 - hop) % size
            names = jnp.where(lane < shots, source * shots + lane, -1)
            return items, attend(0, names, counts, query, items, both, state, False)

        state = attend("own", table, counts, query, [first, second], both, None, False)
        items, state = lax.fori_loop(0, size - 1, shift, ([first, second], state))
        nothing = jnp.full((8, LANES), -1, jnp.int32)
        return attend(0, nothing, counts, query, items, both, state, True)

    attended = lax.cond(
        table[0, STEPS_AT] > STEPS, rest, lambda projected, counts, attended: attended,
        projected, counts, attended,
    )
    mixed = project(attended, w_out, w_parts)
    return mixed


def solution(mesh):
    in_specs = (P("shot", None, None, "head"), P(), P("head", None))
    out_specs = P("shot", None, "head")
    return jax.shard_map(body, mesh=mesh, in_specs=in_specs, out_specs=out_specs, check_vma=False)
```

```python
import functools

import jax
import jax.numpy as jnp
import numpy as np
from jax import lax
from jax.experimental import pallas as pl
from jax.experimental.pallas import tpu as pltpu
from jax.sharding import PartitionSpec as P

HEAD_DIM = 128
ONES = 16
SCALE = float(np.log2(np.e) / np.sqrt(HEAD_DIM))
VMEM_LIMIT = 16 * 1024 * 1024
SIDE = 4
GRID = SIDE * SIDE
LANES = 128
GROUPS = 2
WAYS = 4
STEPS = 5
EARLY_STEPS = STEPS - 1
SEND_AT = 32
FLAG_AT = 64
COUNT_ROW = 1
EARLY_ROW = 3
VMEM = pl.BlockSpec(memory_space=pltpu.VMEM)
SMEM = pl.BlockSpec(memory_space=pltpu.SMEM)
ANY = pl.BlockSpec(memory_space=pl.ANY)
PARAMS = pltpu.CompilerParams(vmem_limit_bytes=VMEM_LIMIT)


def neighbour(index, way):
    x, y = index % SIDE, index // SIDE
    dx, dy = ((-1, 0), (1, 0), (0, -1), (0, 1))[way]
    return (y + dy) % SIDE * SIDE + (x + dx) % SIDE


def permutation(way):
    return [(neighbour(index, way), index) for index in range(GRID)]


def ring(size, stride):
    return [(i, (i + stride) % size) for i in range(size)]


def iota(shape, axis):
    return lax.broadcasted_iota(jnp.int32, shape, axis)


def schedule_kernel(ends_ref, out_ref, rows_ref):
    shots = 2 * GRID
    square = (LANES, LANES)
    stacked = (GROUPS * shots, LANES)
    cube = (GROUPS, shots, LANES)

    def dot(a, b):
        return jnp.dot(
            a.astype(jnp.bfloat16), b.astype(jnp.bfloat16), preferred_element_type=jnp.float32
        )

    def flag(condition):
        return jnp.where(condition, 1.0, 0.0)

    ends, others = ends_ref[0:1, :], ends_ref[1:2, :]
    named = flag(jnp.broadcast_to(ends, (shots, LANES)) == iota((shots, LANES), 0))
    asked = jnp.broadcast_to(others, square)
    holder = 2 * (iota(square, 0) % GRID)
    counts = [
        lax.dot_general(
            named.astype(jnp.bfloat16),
            flag(asked == holder + half).astype(jnp.bfloat16),
            (((1,), (1,)), ((), ())),
            preferred_element_type=jnp.float32,
        )
        for half in range(2)
    ]
    wants = [flag(count > 0.5) for count in counts]
    sizes = [jnp.sum(want, axis=0, keepdims=True) for want in wants]
    second_early = sizes[1] < sizes[0]
    need = jnp.maximum(wants[0], wants[1])
    need_early = jnp.where(second_early, wants[1], wants[0])
    worth = need + need_early

    from_lane, to_lane = iota(square, 0), iota(square, 1)
    same = from_lane // GRID == to_lane // GRID
    dx = (to_lane - from_lane) & (SIDE - 1)
    dy = (to_lane // SIDE - from_lane // SIDE) & (SIDE - 1)
    hops = jnp.where(dx == 3, 1, dx) + jnp.where(dy == 3, 1, dy)
    near = jnp.concatenate([flag(same & (hops == d)) for d in range(1, 5)], axis=1)
    gain = jnp.concatenate([flag(same & (hops < d)) * 2.0**d for d in range(1, 5)], axis=0)
    source = jnp.concatenate(
        [
            flag(same & (dx == a) & (dy == b))
            for a, b in ((1, 0), (SIDE - 1, 0), (0, 1), (0, SIDE - 1))
        ],
        axis=1,
    )
    near, gain, source, group = [a.astype(jnp.bfloat16) for a in (near, gain, source, flag(same))]

    item = iota(cube, 1)
    index = iota(cube, 2) % GRID
    has = flag(item // 2 == index)
    seed = item * 7919 + iota(cube, 2) * 10007 + iota(cube, 0) * 104729
    rows_ref[...] = jnp.full(rows_ref.shape, -1.0, jnp.float32)
    taken = jnp.zeros((GROUPS, 1, LANES), jnp.float32)
    late = jnp.zeros((GROUPS, 1, LANES), jnp.float32)

    def open_groups(held, wanted):
        missing = jnp.max(wanted[None] * (1.0 - held), axis=1, keepdims=True)
        missing = jnp.broadcast_to(missing, (GROUPS, 8, LANES)).reshape(GROUPS * 8, LANES)
        found = jnp.minimum(dot(missing, group), 1.0)
        return found.reshape(GROUPS, 8, LANES)[:, 0:1, :]

    for step in range(STEPS + 1):
        taken = taken + open_groups(has, need)
        if step == EARLY_STEPS:
            late = open_groups(has, need_early)
        if step == STEPS:
            break
        offered = dot(has.reshape(stacked), source)
        held = has
        for way in range(WAYS):
            there = offered[:, way * LANES : (way + 1) * LANES].reshape(cube)
            if step == 0:
                good = (there > 0.5) & (item % 2 == way // 2)
                picked = jnp.min(jnp.where(good, item, shots), axis=1, keepdims=True)
            else:
                reach = dot(held.reshape(stacked), near)
                far = 1.0 - held
                rest = worth[None] * far
                parts = []
                for d in range(4):
                    at = reach[:, d * LANES : (d + 1) * LANES].reshape(cube) > 0.5
                    parts.append(jnp.where(at, rest * far, 0.0).reshape(stacked))
                    far = jnp.where(at, 0.0, far)
                score = dot(jnp.concatenate(parts, axis=1), gain).reshape(cube) + 1.5 * rest
                good = (there > 0.5) & (held < 0.5) & (score > 0.0)
                mixed = seed + (step * WAYS + way) * 31337
                mixed = (mixed ^ (mixed >> 5)) * 40503
                mixed = (mixed ^ (mixed >> 7)) & 4095
                score = jnp.where(good, score + mixed.astype(jnp.float32) * (6.0 / 4096), -1.0)
                best = jnp.max(score, axis=1, keepdims=True)
                picked = jnp.min(
                    jnp.where(good & (score == best), item, shots), axis=1, keepdims=True
                )
            held = jnp.where(item == picked, 1.0, held)
            row = step * WAYS + way
            rows_ref[:, pl.ds(row, 1), :] = jnp.where(picked == shots, -1, picked).astype(
                jnp.float32
            )
        has = held

    flat = iota((GROUPS, 1, LANES), 0) * (LANES // GRID) + iota((GROUPS, 1, LANES), 2) // GRID
    rank = taken + 8.0 * late
    least = jnp.min(jnp.min(rank, axis=2, keepdims=True), axis=0, keepdims=True)
    chosen = jnp.where(rank == least, flat, GROUPS * LANES)
    chosen = jnp.min(jnp.min(chosen, axis=2, keepdims=True), axis=0, keepdims=True)
    rows = jnp.sum(jnp.where(iota((GROUPS, 1, 1), 0) == chosen // (LANES // GRID), rows_ref[...], 0.0), axis=0)
    base = (chosen % (LANES // GRID) * GRID).reshape(1, 1)
    me = lax.axis_index("shot")
    x, y = me % SIDE, me // SIDE
    row, column = iota(rows.shape, 0), iota(rows.shape, 1)
    way = row % WAYS
    target = jnp.where(
        way == 0,
        y * SIDE + (x + 1) % SIDE,
        jnp.where(
            way == 1,
            y * SIDE + (x + SIDE - 1) % SIDE,
            jnp.where(way == 2, (y + 1) % SIDE * SIDE + x, (y + SIDE - 1) % SIDE * SIDE + x),
        ),
    )

    def along_lanes(values, offset):
        return jnp.sum(jnp.where(column == row + offset, values, 0.0), axis=0, keepdims=True)

    got = jnp.sum(jnp.where(column == base + me, rows, 0.0), axis=1, keepdims=True)
    sent = jnp.sum(jnp.where(column == base + target, rows, 0.0), axis=1, keepdims=True)
    lane = iota((1, LANES), 1)
    over = flag(least.reshape(1, 1) > STEPS + 0.5)
    table = along_lanes(got, 0) + along_lanes(sent, SEND_AT) + jnp.where(lane == FLAG_AT, over, 0.0)
    mine = [
        along_lanes(jnp.sum(jnp.where(column == me, count, 0.0), axis=1, keepdims=True), 0)
        for count in counts
    ]
    early = jnp.sum(
        jnp.where(lane == me, flag(second_early), 0.0), axis=1, keepdims=True
    ) + jnp.zeros((1, LANES), jnp.float32)
    blank = jnp.zeros((4, LANES), jnp.float32)
    out_ref[...] = jnp.concatenate([table, *mine, early, blank], axis=0).astype(jnp.int32)


def schedule(pairs):
    first, second = pairs[:, 0], pairs[:, 1]
    ends = jnp.stack([jnp.concatenate([first, second]), jnp.concatenate([second, first])])
    return pl.pallas_call(
        schedule_kernel,
        out_shape=jax.ShapeDtypeStruct((8, LANES), jnp.int32),
        in_specs=[VMEM],
        out_specs=VMEM,
        scratch_shapes=[pltpu.VMEM((GROUPS, 32, LANES), jnp.float32)],
        compiler_params=PARAMS,
        cost_estimate=pl.CostEstimate(
            flops=100_000_000, bytes_accessed=10_000_000, transcendentals=0
        ),
        name="schedule",
    )(ends)


def items_kernel(local_ref, first_ref, second_ref, value_buf, sems):
    out_refs = (first_ref, second_ref)
    keys = [
        pltpu.make_async_copy(local_ref.at[shot, 1], out_refs[shot].at[0], sems.at[shot])
        for shot in range(2)
    ]
    values = [
        pltpu.make_async_copy(local_ref.at[shot, 2], value_buf.at[shot], sems.at[2 + shot])
        for shot in range(2)
    ]
    for copy in values + keys:
        copy.start()
    for shot in range(2):
        values[shot].wait()
        out_refs[shot][1] = value_buf[shot].T
    for copy in keys:
        copy.wait()


def make_items(local):
    shots, _, tokens, width = local.shape
    return pl.pallas_call(
        items_kernel,
        out_shape=[jax.ShapeDtypeStruct((2, width, tokens), local.dtype)] * shots,
        in_specs=[ANY],
        out_specs=[VMEM] * shots,
        scratch_shapes=[
            pltpu.VMEM((shots, tokens, width), local.dtype),
            pltpu.SemaphoreType.DMA((4,)),
        ],
        compiler_params=PARAMS,
        name="items",
    )(local)


def queries_kernel(local_ref, query_ref, buf, sems):
    copies = [
        pltpu.make_async_copy(local_ref.at[shot, 0], buf.at[shot], sems.at[shot])
        for shot in range(2)
    ]
    for copy in copies:
        copy.start()
    for shot in range(2):
        copies[shot].wait()
        query_ref[shot] = buf[shot].T


def make_queries(local):
    shots, _, tokens, width = local.shape
    return pl.pallas_call(
        queries_kernel,
        out_shape=jax.ShapeDtypeStruct((shots, width, tokens), local.dtype),
        in_specs=[ANY],
        out_specs=VMEM,
        scratch_shapes=[
            pltpu.VMEM((shots, tokens, width), local.dtype),
            pltpu.SemaphoreType.DMA((shots,)),
        ],
        compiler_params=PARAMS,
        name="queries",
    )(local)


def attend_kernel(slots, first, ending, later, table_ref, query_ref, *refs):
    count = len(slots)
    item_refs, refs = refs[:count], refs[count:]
    if not first:
        old_acc_ref, old_top_ref, *refs = refs
    refs = refs[later:]
    if ending:
        out_ref, *refs = refs
    acc_ref, top_ref, key_buf, value_buf, sems = refs
    shots, width, tokens = query_ref.shape
    heads = width // HEAD_DIM
    early = table_ref[EARLY_ROW, 0]
    only = ending == "late"

    def copies(slot):
        found = [pltpu.make_async_copy(item_refs[slot].at[0], key_buf.at[slot], sems.at[slot])]
        for head in range(heads):
            found.append(
                pltpu.make_async_copy(
                    item_refs[slot].at[1, pl.ds(head * HEAD_DIM, HEAD_DIM)],
                    value_buf.at[slot, head, pl.ds(0, HEAD_DIM)],
                    sems.at[slot],
                )
            )
        return found

    def times_of(slot, shot):
        kind, at = slots[slot]
        if kind == "own":
            return jnp.where(shot == at, 1, 0)
        item = table_ref[0, at]
        return jnp.where(item >= 0, table_ref[COUNT_ROW + shot, jnp.maximum(item, 0)], 0)

    def used(slot):
        if only:
            return times_of(slot, 1 - early) > 0
        return sum(times_of(slot, shot) for shot in range(shots)) > 0

    for slot in range(count):
        @pl.when(used(slot))
        def _():
            for copy in copies(slot):
                copy.start()

    for slot in range(count):
        for head in range(heads):
            value_buf[slot, head, HEAD_DIM:] = jnp.ones((ONES, tokens), jnp.bfloat16)
    if first:
        acc_ref[...] = jnp.zeros_like(acc_ref)
        top_ref[...] = jnp.full_like(top_ref, -1e30)
    elif only:
        acc_ref[0] = old_acc_ref[1 - early]
        top_ref[0] = old_top_ref[1 - early]
    else:
        acc_ref[...] = old_acc_ref[...]
        top_ref[...] = old_top_ref[...]

    def block(slot, shot, at, times):
        for head in range(heads):
            rows = pl.ds(head * HEAD_DIM, HEAD_DIM)
            scores = jnp.dot(
                key_buf[slot, :, rows], query_ref[shot, rows, :],
                preferred_element_type=jnp.float32,
            )
            old_top = top_ref[at, head, 0:1, :]
            new_top = jnp.maximum(old_top, jnp.max(scores, axis=0, keepdims=True))
            expo = jnp.exp2(scores * SCALE - new_top * SCALE).astype(jnp.bfloat16)
            part = jnp.dot(value_buf[slot, head], expo, preferred_element_type=jnp.float32)
            fade = jnp.exp2((old_top - new_top) * SCALE)
            acc_ref[at, head] = (
                acc_ref[at, head] * fade + part[: HEAD_DIM + 8] * times.astype(jnp.float32)
            )
            top_ref[at, head] = jnp.broadcast_to(new_top, (8, tokens))

    for slot in range(count):
        @pl.when(used(slot))
        def _():
            for copy in copies(slot):
                copy.wait()

            def step(shot, carry):
                times = times_of(slot, shot)

                @pl.when(times > 0)
                def _():
                    block(slot, shot, shot, times)

                return carry

            if only:
                block(slot, 1 - early, 0, times_of(slot, 1 - early))
            else:
                lax.fori_loop(0, shots, step, 0)

    if ending:
        at = 0 if only else early
        for head in range(heads):
            total = acc_ref[at, head, HEAD_DIM : HEAD_DIM + 1, :]
            value = acc_ref[at, head, :HEAD_DIM, :] / total
            out_ref[:, pl.ds(head * HEAD_DIM, HEAD_DIM)] = value.T.astype(out_ref.dtype)


def attend(slots, table, query, items, state=None, ending=None, after=()):
    shots, width, tokens = query.shape
    heads = width // HEAD_DIM
    only = ending == "late"
    kept = 1 if only else shots
    acc = jax.ShapeDtypeStruct((kept, heads, HEAD_DIM + 8, tokens), jnp.float32)
    top = jax.ShapeDtypeStruct((kept, heads, 8, tokens), jnp.float32)
    out = [jax.ShapeDtypeStruct((tokens, width), jnp.bfloat16)] if ending else []
    count = len(slots)
    scratch = [
        pltpu.VMEM((count, tokens, width), jnp.bfloat16),
        pltpu.VMEM((count, heads, HEAD_DIM + ONES, tokens), jnp.bfloat16),
        pltpu.SemaphoreType.DMA((count,)),
    ]
    if only:
        scratch = [pltpu.VMEM(acc.shape, acc.dtype), pltpu.VMEM(top.shape, top.dtype)] + scratch
    else:
        out = out + [acc, top]
    blocks = 2
    return pl.pallas_call(
        functools.partial(attend_kernel, slots, state is None, ending, len(after)),
        out_shape=out,
        in_specs=[SMEM, VMEM]
        + [ANY] * count
        + [VMEM] * (0 if state is None else 2)
        + [ANY] * len(after),
        out_specs=[VMEM] * len(out),
        scratch_shapes=scratch,
        compiler_params=PARAMS,
        cost_estimate=pl.CostEstimate(
            flops=blocks * heads * 4 * tokens * tokens * HEAD_DIM,
            bytes_accessed=count * 2 * width * tokens * 2 + 4 * acc.size * 2,
            transcendentals=blocks * heads * tokens * tokens,
        ),
        name="attend",
    )(table, query, *items, *(() if state is None else state), *after)


def pick_kernel(step, held, table_ref, *refs):
    item_refs, out_refs, sems = refs[:held], refs[-1 - WAYS : -1], refs[-1]
    shots = 2
    me = lax.axis_index("shot")

    def copy(slot, way):
        return pltpu.make_async_copy(item_refs[slot], out_refs[way], sems.at[way])

    wanted = [table_ref[0, SEND_AT + step * WAYS + way] for way in range(WAYS)]
    for slot in range(held):
        item = me * shots + slot if slot < shots else table_ref[0, slot - shots]
        for way in range(WAYS):
            @pl.when((wanted[way] >= 0) & (wanted[way] == item))
            def _():
                copy(slot, way).start()
    for way in range(WAYS):
        @pl.when(wanted[way] >= 0)
        def _():
            copy(0, way).wait()


def pick(step, table, items, after):
    one = jax.ShapeDtypeStruct(items[0].shape, items[0].dtype)
    return pl.pallas_call(
        functools.partial(pick_kernel, step, len(items)),
        out_shape=[one] * WAYS,
        in_specs=[SMEM] + [ANY] * (len(items) + len(after)),
        out_specs=[VMEM] * WAYS,
        scratch_shapes=[pltpu.SemaphoreType.DMA((WAYS,))],
        compiler_params=PARAMS,
        cost_estimate=pl.CostEstimate(
            flops=0, bytes_accessed=2 * WAYS * one.size * 2, transcendentals=0
        ),
        name="pick",
    )(table, *items, *after)


def cut_kernel(count, wide, w_ref, *refs):
    out_refs, sems = refs[-1 - count : -1], refs[-1]
    chip = lax.axis_index("head") // 2
    copies = []
    for move in range(count):
        start = pl.multiple_of((chip + move) % count * wide, HEAD_DIM)
        copies.append(
            pltpu.make_async_copy(w_ref.at[:, pl.ds(start, wide)], out_refs[move], sems.at[move])
        )
    for copy in copies:
        copy.start()
    for copy in copies:
        copy.wait()


def cut_weights(w_out, after):
    chips = lax.axis_size("head") // 2
    depth, wide = w_out.shape[0], w_out.shape[1] // chips
    one = jax.ShapeDtypeStruct((depth, wide), w_out.dtype)
    return pl.pallas_call(
        functools.partial(cut_kernel, chips, wide),
        out_shape=[one] * chips,
        in_specs=[ANY] * (1 + len(after)),
        out_specs=[VMEM] * chips,
        scratch_shapes=[pltpu.SemaphoreType.DMA((chips,))],
        compiler_params=PARAMS,
        cost_estimate=pl.CostEstimate(
            flops=0, bytes_accessed=2 * w_out.size * 2, transcendentals=0
        ),
        name="cut",
    )(w_out, *after)


def along_z(array, move):
    return lax.ppermute(array, "head", ring(lax.axis_size("head"), 2 * move))


def mix_kernel(count, carried, split, *refs):
    rows, weights, refs = refs[:count], refs[count : 2 * count], refs[2 * count :]
    total = None
    if carried:
        total, refs = refs[0][...], refs[1:]
    for row_ref, weight_ref in zip(rows, weights):
        term = jnp.dot(row_ref[...], weight_ref[...], preferred_element_type=jnp.float32)
        total = term if total is None else total + term
    if not split:
        refs[0][...] = total
        return
    keep_ref, give_ref = refs
    half = keep_ref.shape[1]
    first = lax.axis_index("head") % 2 == 0
    low, high = total[:, :half], total[:, half:]
    keep_ref[...] = jnp.where(first, low, high)
    give_ref[...] = jnp.where(first, high, low).astype(give_ref.dtype)


def mix(rows, weights, carry=None, split=True):
    size, wide = rows[0].shape[0], weights[0].shape[1]
    if split:
        out = [
            jax.ShapeDtypeStruct((size, wide // 2), jnp.float32),
            jax.ShapeDtypeStruct((size, wide // 2), jnp.bfloat16),
        ]
    else:
        out = [jax.ShapeDtypeStruct((size, wide), jnp.float32)]
    more = [] if carry is None else [carry]
    return pl.pallas_call(
        functools.partial(mix_kernel, len(rows), carry is not None, split),
        out_shape=out,
        in_specs=[VMEM] * (2 * len(rows) + len(more)),
        out_specs=[VMEM] * len(out),
        compiler_params=PARAMS,
        cost_estimate=pl.CostEstimate(
            flops=2 * len(rows) * rows[0].size * wide,
            bytes_accessed=4 * size * wide,
            transcendentals=0,
        ),
        name="mix",
    )(*rows, *weights, *more)


def swap_cores(give):
    size = lax.axis_size("head")
    return lax.ppermute(give, "head", [(i, i ^ 1) for i in range(size)])


def finish_kernel(table_ref, keep_a, give_a, keep_b, give_b, out_ref):
    early = table_ref[EARLY_ROW, 0]
    out_ref[early] = (keep_a[...] + give_a[...].astype(jnp.float32)).astype(out_ref.dtype)
    out_ref[1 - early] = (keep_b[...] + give_b[...].astype(jnp.float32)).astype(out_ref.dtype)


def finish(table, early, late):
    tokens, part = early[0].shape
    return pl.pallas_call(
        finish_kernel,
        out_shape=jax.ShapeDtypeStruct((2, tokens, part), jnp.bfloat16),
        in_specs=[SMEM] + [VMEM] * 4,
        out_specs=VMEM,
        compiler_params=PARAMS,
        name="finish",
    )(table, *early, *late)


def spread(rows):
    return [rows] + [along_z(rows, move) for move in (1, 3, 2)]


def gather_all(projected, table, w_out):
    me, size = lax.axis_index("shot"), lax.axis_size("shot")
    shots = projected.shape[0]
    local = jnp.transpose(projected, (0, 2, 1, 3))
    query, items = make_queries(local), list(make_items(local))
    lane = jnp.arange(LANES, dtype=jnp.int32)
    both = [("table", 0), ("table", 1)]
    state = attend([("own", 0), ("own", 1)], table, query, items)

    def shift(hop, carry):
        items, state = carry
        items = [lax.ppermute(item, "shot", ring(size, 1)) for item in items]
        source = (me + size - 1 - hop) % size
        names = table.at[0].set(jnp.where(lane < shots, source * shots + lane, -1))
        return items, list(attend(both, names, query, items, state))

    items, state = lax.fori_loop(0, size - 1, shift, (items, list(state)))
    done = table.at[0].set(-1)
    early = attend([], done, query, [], state, "early")[0]
    late = attend([], done, query, [], state, "late")[0]
    own, *parts = cut_weights(w_out, [])
    weights = [own] + [along_z(part, move) for move, part in zip((1, 3, 2), (parts[0], parts[2], parts[1]))]
    sides = []
    for rows in (early, late):
        keep, give = mix(spread(rows), weights)
        sides.append((keep, swap_cores(give)))
    return finish(table, *sides)


def body(projected, pairs, w_out):
    local = jnp.transpose(projected, (0, 2, 1, 3))
    held = list(make_items(local))
    table = schedule(pairs)
    query = make_queries(local)
    state, arrived, weights = None, [], []
    for step in range(STEPS):
        if step == 0:
            outs = (held[0], held[0], held[1], held[1])
        else:
            after = [] if state is None else [state[1]]
            outs = pick(step, table, held, after + weights[step - 2 : step - 1] * (step > 2))
        got = [lax.ppermute(out, "shot", permutation(way)) for way, out in enumerate(outs)]
        slots = [("table", (step - 1) * WAYS + way) for way in range(WAYS)]
        if step == 1:
            state = attend([("own", 0), ("own", 1)] + slots, table, query, held)
            own, near, far, back = cut_weights(w_out, [state[1]])
            weights = [own] + [
                along_z(part, move) for move, part in zip((1, 3, 2), (near, back, far))
            ]
        elif 1 < step < EARLY_STEPS:
            state = attend(slots, table, query, arrived, state)
        elif step == EARLY_STEPS:
            early, *state = attend(slots, table, query, arrived, state, "early", weights[3:])
        arrived = got
        held = held + got

    early_rows = spread(early)
    keep, give = mix(early_rows, weights)
    early_side = (keep, swap_cores(give))
    slots = [("table", (STEPS - 1) * WAYS + way) for way in range(WAYS)]
    late = attend(slots, table, query, arrived, state, "late")[0]
    late_rows = spread(late)
    partial = mix(late_rows[:3], weights[:3], split=False)[0]
    keep, give = mix(late_rows[3:], weights[3:], partial)
    mixed = finish(table, early_side, (keep, swap_cores(give)))
    return lax.cond(
        table[0, FLAG_AT] > 0,
        lambda: gather_all(projected, table, w_out),
        lambda: mixed,
    )


def solution(mesh):
    in_specs = (P("shot", None, None, "head"), P(), P("head", None))
    out_specs = P("shot", None, "head")
    return jax.shard_map(body, mesh=mesh, in_specs=in_specs, out_specs=out_specs, check_vma=False)
```

```python
import functools

import jax
import jax.numpy as jnp
import numpy as np
from jax import lax
from jax.experimental import pallas as pl
from jax.experimental.pallas import tpu as pltpu
from jax.sharding import PartitionSpec as P

HEAD_DIM = 128
SCALE = float(np.log2(np.e) / np.sqrt(HEAD_DIM))
VMEM_LIMIT = 16 * 1024 * 1024
SIDE = 4
GRID = SIDE * SIDE
LANES = 128
GROUPS = 4
WAYS = 4
STEPS = 5
EARLY_STEPS = STEPS - 1
SEND_AT = 32
FLAG_AT = 64
COUNT_ROW = 1
EARLY_ROW = 3
STAY, THERE, BACK, ACROSS = (0, 0), (1, 3), (3, 1), (2, 2)
VMEM = pl.BlockSpec(memory_space=pltpu.VMEM)
SMEM = pl.BlockSpec(memory_space=pltpu.SMEM)
ANY = pl.BlockSpec(memory_space=pl.ANY)
PARAMS = pltpu.CompilerParams(vmem_limit_bytes=VMEM_LIMIT)


def neighbour(index, way):
    x, y = index % SIDE, index // SIDE
    dx, dy = ((-1, 0), (1, 0), (0, -1), (0, 1))[way]
    return (y + dy) % SIDE * SIDE + (x + dx) % SIDE


def permutation(way):
    return [(neighbour(index, way), index) for index in range(GRID)]


def ring(size, stride):
    return [(i, (i + stride) % size) for i in range(size)]


def iota(shape, axis):
    return lax.broadcasted_iota(jnp.int32, shape, axis)


def schedule_kernel(ends_ref, out_ref, rows_ref):
    shots = 2 * GRID
    square = (LANES, LANES)
    stacked = (GROUPS * shots, LANES)
    cube = (GROUPS, shots, LANES)

    def dot(a, b):
        return jnp.dot(
            a.astype(jnp.bfloat16), b.astype(jnp.bfloat16), preferred_element_type=jnp.float32
        )

    def flag(condition):
        return jnp.where(condition, 1.0, 0.0)

    ends, others = ends_ref[0:1, :], ends_ref[1:2, :]
    named = flag(jnp.broadcast_to(ends, (shots, LANES)) == iota((shots, LANES), 0))
    asked = jnp.broadcast_to(others, square)
    holder = 2 * (iota(square, 0) % GRID)
    counts = [
        lax.dot_general(
            named.astype(jnp.bfloat16),
            flag(asked == holder + half).astype(jnp.bfloat16),
            (((1,), (1,)), ((), ())),
            preferred_element_type=jnp.float32,
        )
        for half in range(2)
    ]
    wants = [flag(count > 0.5) for count in counts]
    sizes = [jnp.sum(want, axis=0, keepdims=True) for want in wants]
    second_early = sizes[1] < sizes[0]
    need = jnp.maximum(wants[0], wants[1])
    need_early = jnp.where(second_early, wants[1], wants[0])
    worth = need + need_early

    from_lane, to_lane = iota(square, 0), iota(square, 1)
    same = from_lane // GRID == to_lane // GRID
    dx = (to_lane - from_lane) & (SIDE - 1)
    dy = (to_lane // SIDE - from_lane // SIDE) & (SIDE - 1)
    hops = jnp.where(dx == 3, 1, dx) + jnp.where(dy == 3, 1, dy)
    near = jnp.concatenate([flag(same & (hops == d)) for d in range(1, 5)], axis=1)
    gain = jnp.concatenate([flag(same & (hops < d)) * 2.0**d for d in range(1, 5)], axis=0)
    source = jnp.concatenate(
        [
            flag(same & (dx == a) & (dy == b))
            for a, b in ((1, 0), (SIDE - 1, 0), (0, 1), (0, SIDE - 1))
        ],
        axis=1,
    )
    near, gain, source, group = [a.astype(jnp.bfloat16) for a in (near, gain, source, flag(same))]

    item = iota(cube, 1)
    index = iota(cube, 2) % GRID
    has = flag(item // 2 == index)
    seed = item * 7919 + iota(cube, 2) * 10007 + iota(cube, 0) * 104729
    rows_ref[...] = jnp.full(rows_ref.shape, -1.0, jnp.float32)
    taken = jnp.zeros((GROUPS, 1, LANES), jnp.float32)
    late = jnp.zeros((GROUPS, 1, LANES), jnp.float32)

    def open_groups(held, wanted):
        missing = jnp.max(wanted[None] * (1.0 - held), axis=1, keepdims=True)
        missing = jnp.broadcast_to(missing, (GROUPS, 8, LANES)).reshape(GROUPS * 8, LANES)
        found = jnp.minimum(dot(missing, group), 1.0)
        return found.reshape(GROUPS, 8, LANES)[:, 0:1, :]

    for step in range(STEPS + 1):
        taken = taken + open_groups(has, need)
        if step == EARLY_STEPS:
            late = open_groups(has, need_early)
        if step == STEPS:
            break
        offered = dot(has.reshape(stacked), source)
        held = has
        for way in range(WAYS):
            there = offered[:, way * LANES : (way + 1) * LANES].reshape(cube)
            if step == 0:
                good = (there > 0.5) & (item % 2 == way // 2)
                picked = jnp.min(jnp.where(good, item, shots), axis=1, keepdims=True)
            else:
                reach = dot(held.reshape(stacked), near)
                far = 1.0 - held
                rest = worth[None] * far
                parts = []
                for d in range(4):
                    at = reach[:, d * LANES : (d + 1) * LANES].reshape(cube) > 0.5
                    parts.append(jnp.where(at, rest * far, 0.0).reshape(stacked))
                    far = jnp.where(at, 0.0, far)
                score = dot(jnp.concatenate(parts, axis=1), gain).reshape(cube) + 1.5 * rest
                good = (there > 0.5) & (held < 0.5) & (score > 0.0)
                mixed = seed + (step * WAYS + way) * 31337
                mixed = (mixed ^ (mixed >> 5)) * 40503
                mixed = (mixed ^ (mixed >> 7)) & 4095
                score = jnp.where(good, score + mixed.astype(jnp.float32) * (6.0 / 4096), -1.0)
                best = jnp.max(score, axis=1, keepdims=True)
                picked = jnp.min(
                    jnp.where(good & (score == best), item, shots), axis=1, keepdims=True
                )
            held = jnp.where(item == picked, 1.0, held)
            row = step * WAYS + way
            rows_ref[:, pl.ds(row, 1), :] = jnp.where(picked == shots, -1, picked).astype(
                jnp.float32
            )
        has = held

    flat = iota((GROUPS, 1, LANES), 0) * (LANES // GRID) + iota((GROUPS, 1, LANES), 2) // GRID
    rank = taken + 8.0 * late
    least = jnp.min(jnp.min(rank, axis=2, keepdims=True), axis=0, keepdims=True)
    chosen = jnp.where(rank == least, flat, GROUPS * LANES)
    chosen = jnp.min(jnp.min(chosen, axis=2, keepdims=True), axis=0, keepdims=True)
    rows = jnp.sum(jnp.where(iota((GROUPS, 1, 1), 0) == chosen // (LANES // GRID), rows_ref[...], 0.0), axis=0)
    base = (chosen % (LANES // GRID) * GRID).reshape(1, 1)
    me = lax.axis_index("shot")
    x, y = me % SIDE, me // SIDE
    row, column = iota(rows.shape, 0), iota(rows.shape, 1)
    way = row % WAYS
    target = jnp.where(
        way == 0,
        y * SIDE + (x + 1) % SIDE,
        jnp.where(
            way == 1,
            y * SIDE + (x + SIDE - 1) % SIDE,
            jnp.where(way == 2, (y + 1) % SIDE * SIDE + x, (y + SIDE - 1) % SIDE * SIDE + x),
        ),
    )

    def along_lanes(values, offset):
        return jnp.sum(jnp.where(column == row + offset, values, 0.0), axis=0, keepdims=True)

    got = jnp.sum(jnp.where(column == base + me, rows, 0.0), axis=1, keepdims=True)
    sent = jnp.sum(jnp.where(column == base + target, rows, 0.0), axis=1, keepdims=True)
    lane = iota((1, LANES), 1)
    over = flag(least.reshape(1, 1) > STEPS + 0.5)
    table = along_lanes(got, 0) + along_lanes(sent, SEND_AT) + jnp.where(lane == FLAG_AT, over, 0.0)
    mine = [
        along_lanes(jnp.sum(jnp.where(column == me, count, 0.0), axis=1, keepdims=True), 0)
        for count in counts
    ]
    early = jnp.sum(
        jnp.where(lane == me, flag(second_early), 0.0), axis=1, keepdims=True
    ) + jnp.zeros((1, LANES), jnp.float32)
    blank = jnp.zeros((4, LANES), jnp.float32)
    out_ref[...] = jnp.concatenate([table, *mine, early, blank], axis=0).astype(jnp.int32)


def schedule(pairs):
    first, second = pairs[:, 0], pairs[:, 1]
    ends = jnp.stack([jnp.concatenate([first, second]), jnp.concatenate([second, first])])
    return pl.pallas_call(
        schedule_kernel,
        out_shape=jax.ShapeDtypeStruct((8, LANES), jnp.int32),
        in_specs=[VMEM],
        out_specs=VMEM,
        scratch_shapes=[pltpu.VMEM((GROUPS, 32, LANES), jnp.float32)],
        compiler_params=PARAMS,
        cost_estimate=pl.CostEstimate(
            flops=100_000_000, bytes_accessed=10_000_000, transcendentals=0
        ),
        name="schedule",
    )(ends)


def items_kernel(local_ref, first_ref, second_ref, value_buf, sems):
    out_refs = (first_ref, second_ref)
    keys = [
        pltpu.make_async_copy(local_ref.at[shot, 1], out_refs[shot].at[0], sems.at[shot])
        for shot in range(2)
    ]
    values = [
        pltpu.make_async_copy(local_ref.at[shot, 2], value_buf.at[shot], sems.at[2 + shot])
        for shot in range(2)
    ]
    for copy in values + keys:
        copy.start()
    for shot in range(2):
        values[shot].wait()
        out_refs[shot][1] = value_buf[shot].T
    for copy in keys:
        copy.wait()


def make_items(local):
    shots, _, tokens, width = local.shape
    return pl.pallas_call(
        items_kernel,
        out_shape=[jax.ShapeDtypeStruct((2, width, tokens), local.dtype)] * shots,
        in_specs=[ANY],
        out_specs=[VMEM] * shots,
        scratch_shapes=[
            pltpu.VMEM((shots, tokens, width), local.dtype),
            pltpu.SemaphoreType.DMA((4,)),
        ],
        compiler_params=PARAMS,
        name="items",
    )(local)


def queries_kernel(local_ref, query_ref, buf, sems):
    copies = [
        pltpu.make_async_copy(local_ref.at[shot, 0], buf.at[shot], sems.at[shot])
        for shot in range(2)
    ]
    for copy in copies:
        copy.start()
    for shot in range(2):
        copies[shot].wait()
        query_ref[shot] = buf[shot].T


def make_queries(local):
    shots, _, tokens, width = local.shape
    return pl.pallas_call(
        queries_kernel,
        out_shape=jax.ShapeDtypeStruct((shots, width, tokens), local.dtype),
        in_specs=[ANY],
        out_specs=VMEM,
        scratch_shapes=[
            pltpu.VMEM((shots, tokens, width), local.dtype),
            pltpu.SemaphoreType.DMA((shots,)),
        ],
        compiler_params=PARAMS,
        name="queries",
    )(local)


def attend_kernel(slots, first, which, ending, later, table_ref, query_ref, *refs):
    count = len(slots)
    item_refs, refs = refs[:count], refs[count:]
    if not first:
        old_acc_ref, old_stat_ref, *refs = refs
    refs = refs[later:]
    if ending:
        out_refs, refs = refs[:-2], refs[-2:]
    acc_ref, stat_ref = refs
    shots, width, tokens = query_ref.shape
    heads = width // HEAD_DIM
    early = table_ref[EARLY_ROW, 0]
    chosen = {"early": early, "late": 1 - early}.get(which)

    def times_of(slot, shot):
        kind, at = slots[slot]
        if kind == "own":
            return jnp.where(shot == at, 1, 0)
        item = table_ref[0, at]
        return jnp.where(item >= 0, table_ref[COUNT_ROW + shot, jnp.maximum(item, 0)], 0)

    if first:
        acc_ref[...] = jnp.zeros_like(acc_ref)
        stat_ref[:, :, 0:1, :] = jnp.full_like(stat_ref[:, :, 0:1, :], -1e30)
        stat_ref[:, :, 1:2, :] = jnp.zeros_like(stat_ref[:, :, 1:2, :])
    elif which != "both" and old_acc_ref.shape[0] > 1:
        acc_ref[0] = old_acc_ref[chosen]
        stat_ref[0] = old_stat_ref[chosen]
    else:
        acc_ref[...] = old_acc_ref[...]
        stat_ref[...] = old_stat_ref[...]

    def block(slot, shot, at, times):
        each = range(heads)
        spans = [pl.ds(head * HEAD_DIM, HEAD_DIM) for head in each]
        old = [acc_ref[at, head] for head in each]
        old_top = [stat_ref[at, head, 0:1, :] for head in each]
        old_sum = [stat_ref[at, head, 1:2, :] for head in each]
        weight = times.astype(jnp.float32)
        scores = [
            jnp.dot(
                item_refs[slot][0, :, span], query_ref[shot, span, :],
                preferred_element_type=jnp.float32,
            )
            for span in spans
        ]
        top = [
            jnp.maximum(a, jnp.max(score, axis=0, keepdims=True))
            for a, score in zip(old_top, scores)
        ]
        expo = [jnp.exp2(score * SCALE - a * SCALE) for score, a in zip(scores, top)]
        fade = [jnp.exp2((a - b) * SCALE) for a, b in zip(old_top, top)]
        part = [
            jnp.dot(
                item_refs[slot][1, span, :], e.astype(jnp.bfloat16),
                preferred_element_type=jnp.float32,
            )
            for span, e in zip(spans, expo)
        ]
        total = [jnp.sum(e, axis=0, keepdims=True) for e in expo]
        for head in each:
            acc_ref[at, head] = old[head] * fade[head] + part[head] * weight
            stat_ref[at, head, 0:1, :] = top[head]
            stat_ref[at, head, 1:2, :] = old_sum[head] * fade[head] + total[head] * weight

    for slot in range(count):
        for at in range(shots if which == "both" else 1):
            shot = at if which == "both" else chosen
            if slots[slot][0] == "own":
                if slots[slot][1] == shot:
                    block(slot, shot, at, jnp.int32(1))
                continue
            times = times_of(slot, shot)

            @pl.when(times > 0)
            def _():
                block(slot, shot, at, times)

    if ending:
        for head in range(heads):
            value = acc_ref[0, head] / stat_ref[0, head, 1:2, :]
            value = value.T.astype(jnp.bfloat16)
            size = tokens // len(out_refs)
            for piece, out_ref in enumerate(out_refs):
                out_ref[:, pl.ds(head * HEAD_DIM, HEAD_DIM)] = value[
                    piece * size : (piece + 1) * size
                ]


def attend(slots, table, query, items, state=None, which="both", pieces=0, after=()):
    shots, width, tokens = query.shape
    heads = width // HEAD_DIM
    kept = shots if which == "both" else 1
    acc = jax.ShapeDtypeStruct((kept, heads, HEAD_DIM, tokens), jnp.float32)
    stat = jax.ShapeDtypeStruct((kept, heads, 8, tokens), jnp.float32)
    count = len(slots)
    if pieces:
        out = [jax.ShapeDtypeStruct((tokens // pieces, width), jnp.bfloat16)] * pieces
        scratch = [pltpu.VMEM(acc.shape, acc.dtype), pltpu.VMEM(stat.shape, stat.dtype)]
    else:
        out, scratch = [acc, stat], []
    blocks = 2
    return pl.pallas_call(
        functools.partial(
            attend_kernel, slots, state is None, which, pieces > 0, len(after)
        ),
        out_shape=out,
        in_specs=[SMEM, VMEM]
        + [VMEM] * count
        + [VMEM] * (0 if state is None else 2)
        + [ANY] * len(after),
        out_specs=[VMEM] * len(out),
        scratch_shapes=scratch,
        compiler_params=PARAMS,
        cost_estimate=pl.CostEstimate(
            flops=blocks * heads * 4 * tokens * tokens * HEAD_DIM,
            bytes_accessed=count * 2 * width * tokens * 2 + 4 * acc.size * 2,
            transcendentals=blocks * heads * tokens * tokens,
        ),
        name="attend",
    )(table, query, *items, *(() if state is None else state), *after)


def pick_kernel(step, held, table_ref, *refs):
    item_refs, out_refs, sems = refs[:held], refs[-1 - WAYS : -1], refs[-1]
    shots = 2
    me = lax.axis_index("shot")

    def copy(slot, way):
        return pltpu.make_async_copy(item_refs[slot], out_refs[way], sems.at[way])

    wanted = [table_ref[0, SEND_AT + step * WAYS + way] for way in range(WAYS)]
    for slot in range(held):
        item = me * shots + slot if slot < shots else table_ref[0, slot - shots]
        for way in range(WAYS):
            @pl.when((wanted[way] >= 0) & (wanted[way] == item))
            def _():
                copy(slot, way).start()
    for way in range(WAYS):
        @pl.when(wanted[way] >= 0)
        def _():
            copy(0, way).wait()


def pick(step, table, items, after):
    one = jax.ShapeDtypeStruct(items[0].shape, items[0].dtype)
    return pl.pallas_call(
        functools.partial(pick_kernel, step, len(items)),
        out_shape=[one] * WAYS,
        in_specs=[SMEM] + [ANY] * (len(items) + len(after)),
        out_specs=[VMEM] * WAYS,
        scratch_shapes=[pltpu.SemaphoreType.DMA((WAYS,))],
        compiler_params=PARAMS,
        cost_estimate=pl.CostEstimate(
            flops=0, bytes_accessed=2 * WAYS * one.size * 2, transcendentals=0
        ),
        name="pick",
    )(table, *items, *after)


def cut_kernel(moves, wide, w_ref, *refs):
    out_refs, sems = refs[-1 - len(moves) : -1], refs[-1]
    index = lax.axis_index("head")
    chips = w_ref.shape[1] // wide
    copies = []
    for at, (even, odd) in enumerate(moves):
        chip = (index // 2 + jnp.where(index % 2 == 0, even, odd)) % chips
        start = pl.multiple_of(chip * wide, HEAD_DIM)
        copies.append(
            pltpu.make_async_copy(w_ref.at[:, pl.ds(start, wide)], out_refs[at], sems.at[at])
        )
    for copy in copies:
        copy.start()
    for copy in copies:
        copy.wait()


def cut_weights(w_out, moves, after):
    depth, wide = w_out.shape[0], 2 * (w_out.shape[1] // lax.axis_size("head"))
    one = jax.ShapeDtypeStruct((depth, wide), w_out.dtype)
    return pl.pallas_call(
        functools.partial(cut_kernel, moves, wide),
        out_shape=[one] * len(moves),
        in_specs=[ANY] * (1 + len(after)),
        out_specs=[VMEM] * len(moves),
        scratch_shapes=[pltpu.SemaphoreType.DMA((len(moves),))],
        compiler_params=PARAMS,
        cost_estimate=pl.CostEstimate(
            flops=0, bytes_accessed=4 * len(moves) * one.size, transcendentals=0
        ),
        name="cut",
    )(w_out, *after)


def along_z(array, move):
    size = lax.axis_size("head")
    return lax.ppermute(array, "head", [(i, (i + 2 * move[i % 2]) % size) for i in range(size)])


def mix_kernel(shape, carried, split, *refs):
    count = sum(shape)
    row_refs, weights, refs = refs[:count], refs[count : count + len(shape)], refs[count + len(shape) :]
    total = None
    if carried:
        total, refs = refs[0][...], refs[1:]
    at = 0
    for pieces, weight_ref in zip(shape, weights):
        rows = [ref[...] for ref in row_refs[at : at + pieces]]
        at += pieces
        rows = rows[0] if pieces == 1 else jnp.concatenate(rows, axis=0)
        term = jnp.dot(rows, weight_ref[...], preferred_element_type=jnp.float32)
        total = term if total is None else total + term
    if not split:
        refs[0][...] = total
        return
    keep_ref, give_ref = refs
    half = keep_ref.shape[1]
    first = lax.axis_index("head") % 2 == 0
    low, high = total[:, :half], total[:, half:]
    keep_ref[...] = jnp.where(first, low, high)
    give_ref[...] = jnp.where(first, high, low).astype(give_ref.dtype)


def mix(rows, weights, carry=None, split=True):
    size, wide = sum(piece.shape[0] for piece in rows[0]), weights[0].shape[1]
    if split:
        out = [
            jax.ShapeDtypeStruct((size, wide // 2), jnp.float32),
            jax.ShapeDtypeStruct((size, wide // 2), jnp.bfloat16),
        ]
    else:
        out = [jax.ShapeDtypeStruct((size, wide), jnp.float32)]
    more = [] if carry is None else [carry]
    shape = tuple(len(pieces) for pieces in rows)
    return pl.pallas_call(
        functools.partial(mix_kernel, shape, carry is not None, split),
        out_shape=out,
        in_specs=[VMEM] * (sum(shape) + len(rows) + len(more)),
        out_specs=[VMEM] * len(out),
        compiler_params=PARAMS,
        cost_estimate=pl.CostEstimate(
            flops=2 * len(rows) * size * weights[0].shape[0] * wide,
            bytes_accessed=4 * size * wide,
            transcendentals=0,
        ),
        name="mix",
    )(*(piece for pieces in rows for piece in pieces), *weights, *more)


def swap_cores(give):
    size = lax.axis_size("head")
    return lax.ppermute(give, "head", [(i, i ^ 1) for i in range(size)])


def finish_kernel(table_ref, keep_a, give_a, keep_b, give_b, out_ref):
    early = table_ref[EARLY_ROW, 0]
    out_ref[early] = (keep_a[...] + give_a[...].astype(jnp.float32)).astype(out_ref.dtype)
    out_ref[1 - early] = (keep_b[...] + give_b[...].astype(jnp.float32)).astype(out_ref.dtype)


def finish(table, early, late):
    tokens, part = early[0].shape
    return pl.pallas_call(
        finish_kernel,
        out_shape=jax.ShapeDtypeStruct((2, tokens, part), jnp.bfloat16),
        in_specs=[SMEM] + [VMEM] * 4,
        out_specs=VMEM,
        compiler_params=PARAMS,
        name="finish",
    )(table, *early, *late)


def halve_kernel(first_ref, second_ref, *refs):
    half = first_ref.shape[0] // 2
    refs[-2][...] = first_ref[:half]
    refs[-1][...] = second_ref[half:]


def halve(first, second, after):
    half = jax.ShapeDtypeStruct((first.shape[0] // 2, first.shape[1]), first.dtype)
    return pl.pallas_call(
        halve_kernel,
        out_shape=[half] * 2,
        in_specs=[VMEM] * 2 + [ANY] * len(after),
        out_specs=[VMEM] * 2,
        compiler_params=PARAMS,
        name="halve",
    )(first, second, *after)


def spread_whole(rows, after):
    there, back = along_z(rows, THERE), along_z(rows, BACK)
    upper, lower = halve(there, back, after)
    return [[rows], [there], [back], [along_z(upper, THERE), along_z(lower, BACK)]]


def spread_halves(one, two):
    one_there, two_back = along_z(one, THERE), along_z(two, BACK)
    two_there, one_back = along_z(two, THERE), along_z(one, BACK)
    return [
        [one, two],
        [one_there, two_there],
        [one_back, two_back],
        [along_z(one_there, THERE), along_z(two_back, BACK)],
    ]


def gather_all(projected, table, w_out):
    me, size = lax.axis_index("shot"), lax.axis_size("shot")
    shots = projected.shape[0]
    local = jnp.transpose(projected, (0, 2, 1, 3))
    query, items = make_queries(local), list(make_items(local))
    lane = jnp.arange(LANES, dtype=jnp.int32)
    both = [("table", 0), ("table", 1)]
    state = attend([("own", 0), ("own", 1)], table, query, items)

    def shift(hop, carry):
        items, state = carry
        items = [lax.ppermute(item, "shot", ring(size, 1)) for item in items]
        source = (me + size - 1 - hop) % size
        names = table.at[0].set(jnp.where(lane < shots, source * shots + lane, -1))
        return items, list(attend(both, names, query, items, state))

    items, state = lax.fori_loop(0, size - 1, shift, (items, list(state)))
    done = table.at[0].set(-1)
    early = attend([], done, query, [], state, "early", 1)[0]
    late = attend([], done, query, [], state, "late", 2)
    own, *parts = cut_weights(w_out, (STAY, THERE, BACK, ACROSS), [])
    weights = [own] + [
        along_z(part, move) for part, move in zip(parts, (THERE, BACK, ACROSS))
    ]
    sides = []
    for rows in (spread_whole(early, []), spread_halves(*late)):
        keep, give = mix(rows, weights)
        sides.append((keep, swap_cores(give)))
    return finish(table, *sides)


def body(projected, pairs, w_out):
    local = jnp.transpose(projected, (0, 2, 1, 3))
    held = list(make_items(local))
    table = schedule(pairs)
    query = make_queries(local)
    own, part = cut_weights(w_out, (STAY, THERE), [table])
    weights = [own, along_z(part, THERE)]
    flag = table[0, FLAG_AT]
    state, arrived = None, []
    for step in range(STEPS):
        if step == 0:
            outs = (held[0], held[0], held[1], held[1])
        else:
            after = [query, flag[None]] if state is None else [state[1]]
            outs = pick(step, table, held, after + weights[step - 1 : step] * (step > 1))
        got = [lax.ppermute(out, "shot", permutation(way)) for way, out in enumerate(outs)]
        slots = [("table", (step - 1) * WAYS + way) for way in range(WAYS)]
        if step == 1:
            state = attend([("own", 0), ("own", 1)] + slots, table, query, held)
        elif 1 < step < EARLY_STEPS:
            state = attend(slots, table, query, arrived, state)
        elif step == EARLY_STEPS:
            early = attend(slots, table, query, arrived, state, "early", 1)[0]
            state = attend(slots, table, query, arrived, state, "late", after=[early])
        if step in (1, 2):
            move = (BACK, ACROSS)[step - 1]
            weights.append(along_z(cut_weights(w_out, (move,), [state[1]])[0], move))
        arrived = got
        held = held + got

    slots = [("table", (STEPS - 1) * WAYS + way) for way in range(WAYS)]
    late = attend(slots, table, query, arrived, state, "late", 2)
    keep, give = mix(spread_whole(early, late[:1]), weights)
    early_side = (keep, swap_cores(give))
    late_rows = spread_halves(*late)
    partial = mix(late_rows[:3], weights[:3], split=False)[0]
    keep, give = mix(late_rows[3:], weights[3:], partial)
    late_side = (keep, swap_cores(give))
    return lax.cond(
        flag > 0,
        lambda: gather_all(projected, table, w_out),
        lambda: finish(table, early_side, late_side),
    )


def solution(mesh):
    in_specs = (P("shot", None, None, "head"), P(), P("head", None))
    out_specs = P("shot", None, "head")
    return jax.shard_map(body, mesh=mesh, in_specs=in_specs, out_specs=out_specs, check_vma=False)
```

```python
import functools

import jax
import jax.numpy as jnp
import numpy as np
from jax import lax
from jax.experimental import pallas as pl
from jax.experimental.pallas import tpu as pltpu
from jax.sharding import PartitionSpec as P

HEAD_DIM = 128
SCALE = float(np.log2(np.e) / np.sqrt(HEAD_DIM))
VMEM_LIMIT = 16 * 1024 * 1024
SIDE = 4
GRID = SIDE * SIDE
LANES = 128
GROUPS = 4
WAYS = 4
STEPS = 5
EARLY_STEPS = STEPS - 1
SEND_AT = 32
FLAG_AT = 64
COUNT_ROW = 1
EARLY_ROW = 3
STAY, THERE, BACK, ACROSS = (0, 0), (1, 3), (3, 1), (2, 2)
VMEM = pl.BlockSpec(memory_space=pltpu.VMEM)
SMEM = pl.BlockSpec(memory_space=pltpu.SMEM)
ANY = pl.BlockSpec(memory_space=pl.ANY)
PARAMS = pltpu.CompilerParams(vmem_limit_bytes=VMEM_LIMIT)


def neighbour(index, way):
    x, y = index % SIDE, index // SIDE
    dx, dy = ((-1, 0), (1, 0), (0, -1), (0, 1))[way]
    return (y + dy) % SIDE * SIDE + (x + dx) % SIDE


def permutation(way):
    return [(neighbour(index, way), index) for index in range(GRID)]


def ring(size, stride):
    return [(i, (i + stride) % size) for i in range(size)]


def iota(shape, axis):
    return lax.broadcasted_iota(jnp.int32, shape, axis)


def schedule_kernel(ends_ref, out_ref, rows_ref):
    shots = 2 * GRID
    square = (LANES, LANES)
    stacked = (GROUPS * shots, LANES)
    cube = (GROUPS, shots, LANES)

    def dot(a, b):
        return jnp.dot(
            a.astype(jnp.bfloat16), b.astype(jnp.bfloat16), preferred_element_type=jnp.float32
        )

    def flag(condition):
        return jnp.where(condition, 1.0, 0.0)

    ends, others = ends_ref[0:1, :], ends_ref[1:2, :]
    named = flag(jnp.broadcast_to(ends, (shots, LANES)) == iota((shots, LANES), 0))
    asked = jnp.broadcast_to(others, square)
    holder = 2 * (iota(square, 0) % GRID)
    counts = [
        lax.dot_general(
            named.astype(jnp.bfloat16),
            flag(asked == holder + half).astype(jnp.bfloat16),
            (((1,), (1,)), ((), ())),
            preferred_element_type=jnp.float32,
        )
        for half in range(2)
    ]
    wants = [flag(count > 0.5) for count in counts]
    sizes = [jnp.sum(want, axis=0, keepdims=True) for want in wants]
    second_early = sizes[1] < sizes[0]
    need = jnp.maximum(wants[0], wants[1])
    need_early = jnp.where(second_early, wants[1], wants[0])
    worth = need + need_early

    from_lane, to_lane = iota(square, 0), iota(square, 1)
    same = from_lane // GRID == to_lane // GRID
    dx = (to_lane - from_lane) & (SIDE - 1)
    dy = (to_lane // SIDE - from_lane // SIDE) & (SIDE - 1)
    hops = jnp.where(dx == 3, 1, dx) + jnp.where(dy == 3, 1, dy)
    near = jnp.concatenate([flag(same & (hops == d)) for d in range(1, 5)], axis=1)
    gain = jnp.concatenate([flag(same & (hops < d)) * 2.0**d for d in range(1, 5)], axis=0)
    source = jnp.concatenate(
        [
            flag(same & (dx == a) & (dy == b))
            for a, b in ((1, 0), (SIDE - 1, 0), (0, 1), (0, SIDE - 1))
        ],
        axis=1,
    )
    near, gain, source, group = [a.astype(jnp.bfloat16) for a in (near, gain, source, flag(same))]

    item = iota(cube, 1)
    index = iota(cube, 2) % GRID
    has = flag(item // 2 == index)
    seed = item * 7919 + iota(cube, 2) * 10007 + iota(cube, 0) * 104729
    rows_ref[...] = jnp.full(rows_ref.shape, -1.0, jnp.float32)
    taken = jnp.zeros((GROUPS, 1, LANES), jnp.float32)
    late = jnp.zeros((GROUPS, 1, LANES), jnp.float32)

    def open_groups(held, wanted):
        missing = jnp.max(wanted[None] * (1.0 - held), axis=1, keepdims=True)
        missing = jnp.broadcast_to(missing, (GROUPS, 8, LANES)).reshape(GROUPS * 8, LANES)
        found = jnp.minimum(dot(missing, group), 1.0)
        return found.reshape(GROUPS, 8, LANES)[:, 0:1, :]

    for step in range(STEPS + 1):
        taken = taken + open_groups(has, need)
        if step == EARLY_STEPS:
            late = open_groups(has, need_early)
        if step == STEPS:
            break
        offered = dot(has.reshape(stacked), source)
        held = has
        for way in range(WAYS):
            there = offered[:, way * LANES : (way + 1) * LANES].reshape(cube)
            if step == 0:
                good = (there > 0.5) & (item % 2 == way // 2)
                picked = jnp.min(jnp.where(good, item, shots), axis=1, keepdims=True)
            else:
                reach = dot(held.reshape(stacked), near)
                far = 1.0 - held
                rest = worth[None] * far
                parts = []
                for d in range(4):
                    at = reach[:, d * LANES : (d + 1) * LANES].reshape(cube) > 0.5
                    parts.append(jnp.where(at, rest * far, 0.0).reshape(stacked))
                    far = jnp.where(at, 0.0, far)
                score = dot(jnp.concatenate(parts, axis=1), gain).reshape(cube) + 1.5 * rest
                good = (there > 0.5) & (held < 0.5) & (score > 0.0)
                mixed = seed + (step * WAYS + way) * 31337
                mixed = (mixed ^ (mixed >> 5)) * 40503
                mixed = (mixed ^ (mixed >> 7)) & 4095
                score = jnp.where(good, score + mixed.astype(jnp.float32) * (6.0 / 4096), -1.0)
                best = jnp.max(score, axis=1, keepdims=True)
                picked = jnp.min(
                    jnp.where(good & (score == best), item, shots), axis=1, keepdims=True
                )
            held = jnp.where(item == picked, 1.0, held)
            row = step * WAYS + way
            rows_ref[:, pl.ds(row, 1), :] = jnp.where(picked == shots, -1, picked).astype(
                jnp.float32
            )
        has = held

    flat = iota((GROUPS, 1, LANES), 0) * (LANES // GRID) + iota((GROUPS, 1, LANES), 2) // GRID
    rank = taken + 8.0 * late
    least = jnp.min(jnp.min(rank, axis=2, keepdims=True), axis=0, keepdims=True)
    chosen = jnp.where(rank == least, flat, GROUPS * LANES)
    chosen = jnp.min(jnp.min(chosen, axis=2, keepdims=True), axis=0, keepdims=True)
    rows = jnp.sum(jnp.where(iota((GROUPS, 1, 1), 0) == chosen // (LANES // GRID), rows_ref[...], 0.0), axis=0)
    base = (chosen % (LANES // GRID) * GRID).reshape(1, 1)
    me = lax.axis_index("shot")
    x, y = me % SIDE, me // SIDE
    row, column = iota(rows.shape, 0), iota(rows.shape, 1)
    way = row % WAYS
    target = jnp.where(
        way == 0,
        y * SIDE + (x + 1) % SIDE,
        jnp.where(
            way == 1,
            y * SIDE + (x + SIDE - 1) % SIDE,
            jnp.where(way == 2, (y + 1) % SIDE * SIDE + x, (y + SIDE - 1) % SIDE * SIDE + x),
        ),
    )

    def along_lanes(values, offset):
        return jnp.sum(jnp.where(column == row + offset, values, 0.0), axis=0, keepdims=True)

    got = jnp.sum(jnp.where(column == base + me, rows, 0.0), axis=1, keepdims=True)
    sent = jnp.sum(jnp.where(column == base + target, rows, 0.0), axis=1, keepdims=True)
    lane = iota((1, LANES), 1)
    over = flag(least.reshape(1, 1) > STEPS + 0.5)
    table = along_lanes(got, 0) + along_lanes(sent, SEND_AT) + jnp.where(lane == FLAG_AT, over, 0.0)
    mine = [
        along_lanes(jnp.sum(jnp.where(column == me, count, 0.0), axis=1, keepdims=True), 0)
        for count in counts
    ]
    early = jnp.sum(
        jnp.where(lane == me, flag(second_early), 0.0), axis=1, keepdims=True
    ) + jnp.zeros((1, LANES), jnp.float32)
    blank = jnp.zeros((4, LANES), jnp.float32)
    out_ref[...] = jnp.concatenate([table, *mine, early, blank], axis=0).astype(jnp.int32)


def schedule(pairs):
    first, second = pairs[:, 0], pairs[:, 1]
    ends = jnp.stack([jnp.concatenate([first, second]), jnp.concatenate([second, first])])
    return pl.pallas_call(
        schedule_kernel,
        out_shape=jax.ShapeDtypeStruct((8, LANES), jnp.int32),
        in_specs=[VMEM],
        out_specs=VMEM,
        scratch_shapes=[pltpu.VMEM((GROUPS, 32, LANES), jnp.float32)],
        compiler_params=PARAMS,
        cost_estimate=pl.CostEstimate(
            flops=100_000_000, bytes_accessed=10_000_000, transcendentals=0
        ),
        name="schedule",
    )(ends)


def items_kernel(local_ref, first_ref, second_ref, value_buf, sems):
    out_refs = (first_ref, second_ref)
    keys = [
        pltpu.make_async_copy(local_ref.at[shot, 1], out_refs[shot].at[0], sems.at[shot])
        for shot in range(2)
    ]
    values = [
        pltpu.make_async_copy(local_ref.at[shot, 2], value_buf.at[shot], sems.at[2 + shot])
        for shot in range(2)
    ]
    for copy in values + keys:
        copy.start()
    for shot in range(2):
        values[shot].wait()
        out_refs[shot][1] = value_buf[shot].T
    for copy in keys:
        copy.wait()


def make_items(local):
    shots, _, tokens, width = local.shape
    return pl.pallas_call(
        items_kernel,
        out_shape=[jax.ShapeDtypeStruct((2, width, tokens), local.dtype)] * shots,
        in_specs=[ANY],
        out_specs=[VMEM] * shots,
        scratch_shapes=[
            pltpu.VMEM((shots, tokens, width), local.dtype),
            pltpu.SemaphoreType.DMA((4,)),
        ],
        compiler_params=PARAMS,
        name="items",
    )(local)


def queries_kernel(local_ref, query_ref, buf, sems):
    copies = [
        pltpu.make_async_copy(local_ref.at[shot, 0], buf.at[shot], sems.at[shot])
        for shot in range(2)
    ]
    for copy in copies:
        copy.start()
    for shot in range(2):
        copies[shot].wait()
        query_ref[shot] = buf[shot].T


def make_queries(local):
    shots, _, tokens, width = local.shape
    return pl.pallas_call(
        queries_kernel,
        out_shape=jax.ShapeDtypeStruct((shots, width, tokens), local.dtype),
        in_specs=[ANY],
        out_specs=VMEM,
        scratch_shapes=[
            pltpu.VMEM((shots, tokens, width), local.dtype),
            pltpu.SemaphoreType.DMA((shots,)),
        ],
        compiler_params=PARAMS,
        name="queries",
    )(local)


def attend_kernel(slots, first, which, ending, later, table_ref, query_ref, *refs):
    count = len(slots)
    item_refs, refs = refs[:count], refs[count:]
    if not first:
        old_acc_ref, old_stat_ref, *refs = refs
    refs = refs[later:]
    if ending:
        out_refs, refs = refs[:-2], refs[-2:]
    acc_ref, stat_ref = refs
    shots, width, tokens = query_ref.shape
    heads = width // HEAD_DIM
    early = table_ref[EARLY_ROW, 0]
    chosen = {"early": early, "late": 1 - early}.get(which)

    def times_of(slot, shot):
        kind, at = slots[slot]
        if kind == "own":
            return jnp.where(shot == at, 1, 0)
        item = table_ref[0, at]
        return jnp.where(item >= 0, table_ref[COUNT_ROW + shot, jnp.maximum(item, 0)], 0)

    if first:
        acc_ref[...] = jnp.zeros_like(acc_ref)
        stat_ref[:, :, 0:1, :] = jnp.full_like(stat_ref[:, :, 0:1, :], -1e30)
        stat_ref[:, :, 1:2, :] = jnp.zeros_like(stat_ref[:, :, 1:2, :])
    elif which != "both" and old_acc_ref.shape[0] > 1:
        acc_ref[0] = old_acc_ref[chosen]
        stat_ref[0] = old_stat_ref[chosen]
    else:
        acc_ref[...] = old_acc_ref[...]
        stat_ref[...] = old_stat_ref[...]

    def block(slot, shot, at, times):
        each = range(heads)
        spans = [pl.ds(head * HEAD_DIM, HEAD_DIM) for head in each]
        old = [acc_ref[at, head] for head in each]
        old_top = [stat_ref[at, head, 0:1, :] for head in each]
        old_sum = [stat_ref[at, head, 1:2, :] for head in each]
        weight = times.astype(jnp.float32)
        scores = [
            jnp.dot(
                item_refs[slot][0, :, span], query_ref[shot, span, :],
                preferred_element_type=jnp.float32,
            )
            for span in spans
        ]
        top = [
            jnp.maximum(a, jnp.max(score, axis=0, keepdims=True))
            for a, score in zip(old_top, scores)
        ]
        expo = [jnp.exp2(score * SCALE - a * SCALE) for score, a in zip(scores, top)]
        fade = [jnp.exp2((a - b) * SCALE) for a, b in zip(old_top, top)]
        part = [
            jnp.dot(
                item_refs[slot][1, span, :], e.astype(jnp.bfloat16),
                preferred_element_type=jnp.float32,
            )
            for span, e in zip(spans, expo)
        ]
        total = [jnp.sum(e, axis=0, keepdims=True) for e in expo]
        for head in each:
            acc_ref[at, head] = old[head] * fade[head] + part[head] * weight
            stat_ref[at, head, 0:1, :] = top[head]
            stat_ref[at, head, 1:2, :] = old_sum[head] * fade[head] + total[head] * weight

    for slot in range(count):
        for at in range(shots if which == "both" else 1):
            shot = at if which == "both" else chosen
            if slots[slot][0] == "own":
                if slots[slot][1] == shot:
                    block(slot, shot, at, jnp.int32(1))
                continue
            times = times_of(slot, shot)

            @pl.when(times > 0)
            def _():
                block(slot, shot, at, times)

    if ending:
        for head in range(heads):
            value = acc_ref[0, head] / stat_ref[0, head, 1:2, :]
            value = value.T.astype(jnp.bfloat16)
            size = tokens // len(out_refs)
            for piece, out_ref in enumerate(out_refs):
                out_ref[:, pl.ds(head * HEAD_DIM, HEAD_DIM)] = value[
                    piece * size : (piece + 1) * size
                ]


def attend(slots, table, query, items, state=None, which="both", pieces=0, after=()):
    shots, width, tokens = query.shape
    heads = width // HEAD_DIM
    kept = shots if which == "both" else 1
    acc = jax.ShapeDtypeStruct((kept, heads, HEAD_DIM, tokens), jnp.float32)
    stat = jax.ShapeDtypeStruct((kept, heads, 8, tokens), jnp.float32)
    count = len(slots)
    if pieces:
        out = [jax.ShapeDtypeStruct((tokens // pieces, width), jnp.bfloat16)] * pieces
        scratch = [pltpu.VMEM(acc.shape, acc.dtype), pltpu.VMEM(stat.shape, stat.dtype)]
    else:
        out, scratch = [acc, stat], []
    blocks = 2
    return pl.pallas_call(
        functools.partial(
            attend_kernel, slots, state is None, which, pieces > 0, len(after)
        ),
        out_shape=out,
        in_specs=[SMEM, VMEM]
        + [VMEM] * count
        + [VMEM] * (0 if state is None else 2)
        + [ANY] * len(after),
        out_specs=[VMEM] * len(out),
        scratch_shapes=scratch,
        compiler_params=PARAMS,
        cost_estimate=pl.CostEstimate(
            flops=blocks * heads * 4 * tokens * tokens * HEAD_DIM,
            bytes_accessed=count * 2 * width * tokens * 2 + 4 * acc.size * 2,
            transcendentals=blocks * heads * tokens * tokens,
        ),
        name="attend",
    )(table, query, *items, *(() if state is None else state), *after)


def pick_kernel(step, held, table_ref, *refs):
    item_refs, out_refs, sems = refs[:held], refs[-1 - WAYS : -1], refs[-1]
    shots = 2
    me = lax.axis_index("shot")

    def copy(slot, way):
        return pltpu.make_async_copy(item_refs[slot], out_refs[way], sems.at[way])

    wanted = [table_ref[0, SEND_AT + step * WAYS + way] for way in range(WAYS)]
    for slot in range(held):
        item = me * shots + slot if slot < shots else table_ref[0, slot - shots]
        for way in range(WAYS):
            @pl.when((wanted[way] >= 0) & (wanted[way] == item))
            def _():
                copy(slot, way).start()
    for way in range(WAYS):
        @pl.when(wanted[way] >= 0)
        def _():
            copy(0, way).wait()


def pick(step, table, items, after):
    one = jax.ShapeDtypeStruct(items[0].shape, items[0].dtype)
    return pl.pallas_call(
        functools.partial(pick_kernel, step, len(items)),
        out_shape=[one] * WAYS,
        in_specs=[SMEM] + [ANY] * (len(items) + len(after)),
        out_specs=[VMEM] * WAYS,
        scratch_shapes=[pltpu.SemaphoreType.DMA((WAYS,))],
        compiler_params=PARAMS,
        cost_estimate=pl.CostEstimate(
            flops=0, bytes_accessed=2 * WAYS * one.size * 2, transcendentals=0
        ),
        name="pick",
    )(table, *items, *after)


def cut_kernel(moves, wide, w_ref, *refs):
    out_refs, sems = refs[-1 - len(moves) : -1], refs[-1]
    index = lax.axis_index("head")
    chips = w_ref.shape[1] // wide
    copies = []
    for at, (even, odd) in enumerate(moves):
        chip = (index // 2 + jnp.where(index % 2 == 0, even, odd)) % chips
        start = pl.multiple_of(chip * wide, HEAD_DIM)
        copies.append(
            pltpu.make_async_copy(w_ref.at[:, pl.ds(start, wide)], out_refs[at], sems.at[at])
        )
    for copy in copies:
        copy.start()
    for copy in copies:
        copy.wait()


def cut_weights(w_out, moves, after):
    depth, wide = w_out.shape[0], 2 * (w_out.shape[1] // lax.axis_size("head"))
    one = jax.ShapeDtypeStruct((depth, wide), w_out.dtype)
    return pl.pallas_call(
        functools.partial(cut_kernel, moves, wide),
        out_shape=[one] * len(moves),
        in_specs=[ANY] * (1 + len(after)),
        out_specs=[VMEM] * len(moves),
        scratch_shapes=[pltpu.SemaphoreType.DMA((len(moves),))],
        compiler_params=PARAMS,
        cost_estimate=pl.CostEstimate(
            flops=0, bytes_accessed=4 * len(moves) * one.size, transcendentals=0
        ),
        name="cut",
    )(w_out, *after)


def along_z(array, move):
    size = lax.axis_size("head")
    return lax.ppermute(array, "head", [(i, (i + 2 * move[i % 2]) % size) for i in range(size)])


def mix_kernel(shape, carried, split, *refs):
    count = sum(shape)
    row_refs, weights, refs = refs[:count], refs[count : count + len(shape)], refs[count + len(shape) :]
    total = None
    if carried:
        total, refs = refs[0][...], refs[1:]
    at = 0
    for pieces, weight_ref in zip(shape, weights):
        rows = [ref[...] for ref in row_refs[at : at + pieces]]
        at += pieces
        rows = rows[0] if pieces == 1 else jnp.concatenate(rows, axis=0)
        term = jnp.dot(rows, weight_ref[...], preferred_element_type=jnp.float32)
        total = term if total is None else total + term
    if not split:
        refs[0][...] = total
        return
    keep_ref, give_ref = refs
    half = keep_ref.shape[1]
    first = lax.axis_index("head") % 2 == 0
    low, high = total[:, :half], total[:, half:]
    keep_ref[...] = jnp.where(first, low, high)
    give_ref[...] = jnp.where(first, high, low).astype(give_ref.dtype)


def mix(rows, weights, carry=None, split=True):
    size, wide = sum(piece.shape[0] for piece in rows[0]), weights[0].shape[1]
    if split:
        out = [
            jax.ShapeDtypeStruct((size, wide // 2), jnp.float32),
            jax.ShapeDtypeStruct((size, wide // 2), jnp.bfloat16),
        ]
    else:
        out = [jax.ShapeDtypeStruct((size, wide), jnp.float32)]
    more = [] if carry is None else [carry]
    shape = tuple(len(pieces) for pieces in rows)
    return pl.pallas_call(
        functools.partial(mix_kernel, shape, carry is not None, split),
        out_shape=out,
        in_specs=[VMEM] * (sum(shape) + len(rows) + len(more)),
        out_specs=[VMEM] * len(out),
        compiler_params=PARAMS,
        cost_estimate=pl.CostEstimate(
            flops=2 * len(rows) * size * weights[0].shape[0] * wide,
            bytes_accessed=4 * size * wide,
            transcendentals=0,
        ),
        name="mix",
    )(*(piece for pieces in rows for piece in pieces), *weights, *more)


def swap_cores(give):
    size = lax.axis_size("head")
    return lax.ppermute(give, "head", [(i, i ^ 1) for i in range(size)])


def finish_kernel(table_ref, keep_a, give_a, keep_b, give_b, out_ref):
    early = table_ref[EARLY_ROW, 0]
    out_ref[early] = (keep_a[...] + give_a[...].astype(jnp.float32)).astype(out_ref.dtype)
    out_ref[1 - early] = (keep_b[...] + give_b[...].astype(jnp.float32)).astype(out_ref.dtype)


def finish(table, early, late):
    tokens, part = early[0].shape
    return pl.pallas_call(
        finish_kernel,
        out_shape=jax.ShapeDtypeStruct((2, tokens, part), jnp.bfloat16),
        in_specs=[SMEM] + [VMEM] * 4,
        out_specs=VMEM,
        compiler_params=PARAMS,
        name="finish",
    )(table, *early, *late)


def halve_kernel(first_ref, second_ref, *refs):
    half = first_ref.shape[0] // 2
    refs[-2][...] = first_ref[:half]
    refs[-1][...] = second_ref[half:]


def halve(first, second, after):
    half = jax.ShapeDtypeStruct((first.shape[0] // 2, first.shape[1]), first.dtype)
    return pl.pallas_call(
        halve_kernel,
        out_shape=[half] * 2,
        in_specs=[VMEM] * 2 + [ANY] * len(after),
        out_specs=[VMEM] * 2,
        compiler_params=PARAMS,
        name="halve",
    )(first, second, *after)


def spread_whole(rows, after):
    there, back = along_z(rows, THERE), along_z(rows, BACK)
    upper, lower = halve(there, back, after)
    return [[rows], [there], [back], [along_z(upper, THERE), along_z(lower, BACK)]]


def spread_halves(one, two):
    one_there, two_back = along_z(one, THERE), along_z(two, BACK)
    two_there, one_back = along_z(two, THERE), along_z(one, BACK)
    return [
        [one, two],
        [one_there, two_there],
        [one_back, two_back],
        [along_z(one_there, THERE), along_z(two_back, BACK)],
    ]


def gather_all(projected, table, w_out):
    me, size = lax.axis_index("shot"), lax.axis_size("shot")
    shots = projected.shape[0]
    local = jnp.transpose(projected, (0, 2, 1, 3))
    query, items = make_queries(local), list(make_items(local))
    lane = jnp.arange(LANES, dtype=jnp.int32)
    both = [("table", 0), ("table", 1)]
    state = attend([("own", 0), ("own", 1)], table, query, items)

    def shift(hop, carry):
        items, state = carry
        items = [lax.ppermute(item, "shot", ring(size, 1)) for item in items]
        source = (me + size - 1 - hop) % size
        names = table.at[0].set(jnp.where(lane < shots, source * shots + lane, -1))
        return items, list(attend(both, names, query, items, state))

    items, state = lax.fori_loop(0, size - 1, shift, (items, list(state)))
    done = table.at[0].set(-1)
    early = attend([], done, query, [], state, "early", 1)[0]
    late = attend([], done, query, [], state, "late", 2)
    own, *parts = cut_weights(w_out, (STAY, THERE, BACK, ACROSS), [])
    weights = [own] + [
        along_z(part, move) for part, move in zip(parts, (THERE, BACK, ACROSS))
    ]
    sides = []
    for rows in (spread_whole(early, []), spread_halves(*late)):
        keep, give = mix(rows, weights)
        sides.append((keep, swap_cores(give)))
    return finish(table, *sides)


def body(projected, pairs, w_out):
    local = jnp.transpose(projected, (0, 2, 1, 3))
    held = list(make_items(local))
    table = schedule(pairs)
    query = make_queries(local)
    own, part = cut_weights(w_out, (STAY, THERE), [table])
    weights = [own, along_z(part, THERE)]
    flag = table[0, FLAG_AT]
    state, arrived = None, []
    for step in range(STEPS):
        if step == 0:
            outs = (held[0], held[0], held[1], held[1])
        else:
            after = [query, flag[None]] if state is None else [state[1]]
            outs = pick(step, table, held, after + weights[step - 1 : step] * (step > 1))
        got = [lax.ppermute(out, "shot", permutation(way)) for way, out in enumerate(outs)]
        slots = [("table", (step - 1) * WAYS + way) for way in range(WAYS)]
        if step == 1:
            state = attend(slots, table, query, arrived)
        elif 1 < step < EARLY_STEPS:
            own_slots = [("own", 0), ("own", 1)] * (step == EARLY_STEPS - 1)
            state = attend(own_slots + slots, table, query, held[: len(own_slots)] + arrived, state)
        elif step == EARLY_STEPS:
            early = attend(slots, table, query, arrived, state, "early", 1)[0]
            state = attend(slots, table, query, arrived, state, "late", after=[early])
        if step in (1, 2):
            move = (BACK, ACROSS)[step - 1]
            weights.append(along_z(cut_weights(w_out, (move,), [state[1]])[0], move))
        arrived = got
        held = held + got

    slots = [("table", (STEPS - 1) * WAYS + way) for way in range(WAYS)]
    late = attend(slots, table, query, arrived, state, "late", 1)[0]
    keep, give = mix(spread_whole(early, [late]), weights)
    early_side = (keep, swap_cores(give))
    late_rows = spread_whole(late, [])
    partial = mix(late_rows[:3], weights[:3], split=False)[0]
    keep, give = mix(late_rows[3:], weights[3:], partial)
    late_side = (keep, swap_cores(give))
    return lax.cond(
        flag > 0,
        lambda: gather_all(projected, table, w_out),
        lambda: finish(table, early_side, late_side),
    )


def solution(mesh):
    in_specs = (P("shot", None, None, "head"), P(), P("head", None))
    out_specs = P("shot", None, "head")
    return jax.shard_map(body, mesh=mesh, in_specs=in_specs, out_specs=out_specs, check_vma=False)
```

```python
import functools

import jax
import jax.numpy as jnp
import numpy as np
from jax import lax
from jax.experimental import pallas as pl
from jax.experimental.pallas import tpu as pltpu
from jax.sharding import PartitionSpec as P

HEAD_DIM = 128
SCALE = float(np.log2(np.e) / np.sqrt(HEAD_DIM))
VMEM_LIMIT = 16 * 1024 * 1024
SIDE = 4
GRID = SIDE * SIDE
LANES = 128
GROUPS = 4
WAYS = 4
PARTNER = (1, 3, SIDE, 3 * SIDE)
STEPS = 5
EARLY_STEPS = STEPS - 1
SEND_AT = 32
FLAG_AT = 64
COUNT_ROW = 1
EARLY_ROW = 3
STAY, THERE, BACK, ACROSS = (0, 0), (1, 3), (3, 1), (2, 2)
VMEM = pl.BlockSpec(memory_space=pltpu.VMEM)
SMEM = pl.BlockSpec(memory_space=pltpu.SMEM)
ANY = pl.BlockSpec(memory_space=pl.ANY)
PARAMS = pltpu.CompilerParams(vmem_limit_bytes=VMEM_LIMIT)


def permutation(way):
    return [(index, index ^ PARTNER[way]) for index in range(GRID)]


def ring(size, stride):
    return [(i, (i + stride) % size) for i in range(size)]


def iota(shape, axis):
    return lax.broadcasted_iota(jnp.int32, shape, axis)


def schedule_kernel(ends_ref, out_ref, rows_ref):
    shots = 2 * GRID
    square = (LANES, LANES)
    stacked = (GROUPS * shots, LANES)
    cube = (GROUPS, shots, LANES)

    def dot(a, b):
        return jnp.dot(
            a.astype(jnp.bfloat16), b.astype(jnp.bfloat16), preferred_element_type=jnp.float32
        )

    def flag(condition):
        return jnp.where(condition, 1.0, 0.0)

    ends, others = ends_ref[0:1, :], ends_ref[1:2, :]
    named = flag(jnp.broadcast_to(ends, (shots, LANES)) == iota((shots, LANES), 0))
    asked = jnp.broadcast_to(others, square)
    holder = 2 * (iota(square, 0) % GRID)
    counts = [
        lax.dot_general(
            named.astype(jnp.bfloat16),
            flag(asked == holder + half).astype(jnp.bfloat16),
            (((1,), (1,)), ((), ())),
            preferred_element_type=jnp.float32,
        )
        for half in range(2)
    ]
    wants = [flag(count > 0.5) for count in counts]
    sizes = [jnp.sum(want, axis=0, keepdims=True) for want in wants]
    second_early = sizes[1] < sizes[0]
    need = jnp.maximum(wants[0], wants[1])
    need_early = jnp.where(second_early, wants[1], wants[0])
    worth = need + need_early

    from_lane, to_lane = iota(square, 0), iota(square, 1)
    same = from_lane // GRID == to_lane // GRID
    dx = (to_lane - from_lane) & (SIDE - 1)
    dy = (to_lane // SIDE - from_lane // SIDE) & (SIDE - 1)
    hops = jnp.where(dx == 3, 1, dx) + jnp.where(dy == 3, 1, dy)
    near = jnp.concatenate([flag(same & (hops == d)) for d in range(1, 5)], axis=1)
    gain = jnp.concatenate([flag(same & (hops < d)) * 2.0**d for d in range(1, 5)], axis=0)
    source = jnp.concatenate(
        [flag(from_lane == to_lane ^ partner) for partner in PARTNER], axis=1
    )
    near, gain, source, group = [a.astype(jnp.bfloat16) for a in (near, gain, source, flag(same))]

    item = iota(cube, 1)
    index = iota(cube, 2) % GRID
    has = flag(item // 2 == index)
    seed = item * 7919 + iota(cube, 2) * 10007 + iota(cube, 0) * 104729
    rows_ref[...] = jnp.full(rows_ref.shape, -1.0, jnp.float32)
    taken = jnp.zeros((GROUPS, 1, LANES), jnp.float32)
    late = jnp.zeros((GROUPS, 1, LANES), jnp.float32)

    def open_groups(held, wanted):
        missing = jnp.max(wanted[None] * (1.0 - held), axis=1, keepdims=True)
        missing = jnp.broadcast_to(missing, (GROUPS, 8, LANES)).reshape(GROUPS * 8, LANES)
        found = jnp.minimum(dot(missing, group), 1.0)
        return found.reshape(GROUPS, 8, LANES)[:, 0:1, :]

    for step in range(STEPS + 1):
        taken = taken + open_groups(has, need)
        if step == EARLY_STEPS:
            late = open_groups(has, need_early)
        if step == STEPS:
            break
        offered = dot(has.reshape(stacked), source)
        held = has
        for way in range(WAYS):
            there = offered[:, way * LANES : (way + 1) * LANES].reshape(cube)
            if step == 0:
                good = (there > 0.5) & (item % 2 == way // 2)
                picked = jnp.min(jnp.where(good, item, shots), axis=1, keepdims=True)
            else:
                reach = dot(held.reshape(stacked), near)
                far = 1.0 - held
                rest = worth[None] * far
                parts = []
                for d in range(4):
                    at = reach[:, d * LANES : (d + 1) * LANES].reshape(cube) > 0.5
                    parts.append(jnp.where(at, rest * far, 0.0).reshape(stacked))
                    far = jnp.where(at, 0.0, far)
                score = dot(jnp.concatenate(parts, axis=1), gain).reshape(cube) + 1.5 * rest
                good = (there > 0.5) & (held < 0.5) & (score > 0.0)
                mixed = seed + (step * WAYS + way) * 31337
                mixed = (mixed ^ (mixed >> 5)) * 40503
                mixed = (mixed ^ (mixed >> 7)) & 4095
                score = jnp.where(good, score + mixed.astype(jnp.float32) * (6.0 / 4096), -1.0)
                best = jnp.max(score, axis=1, keepdims=True)
                picked = jnp.min(
                    jnp.where(good & (score == best), item, shots), axis=1, keepdims=True
                )
            held = jnp.where(item == picked, 1.0, held)
            row = step * WAYS + way
            rows_ref[:, pl.ds(row, 1), :] = jnp.where(picked == shots, -1, picked).astype(
                jnp.float32
            )
        has = held

    flat = iota((GROUPS, 1, LANES), 0) * (LANES // GRID) + iota((GROUPS, 1, LANES), 2) // GRID
    rank = taken + 8.0 * late
    least = jnp.min(jnp.min(rank, axis=2, keepdims=True), axis=0, keepdims=True)
    chosen = jnp.where(rank == least, flat, GROUPS * LANES)
    chosen = jnp.min(jnp.min(chosen, axis=2, keepdims=True), axis=0, keepdims=True)
    rows = jnp.sum(jnp.where(iota((GROUPS, 1, 1), 0) == chosen // (LANES // GRID), rows_ref[...], 0.0), axis=0)
    base = (chosen % (LANES // GRID) * GRID).reshape(1, 1)
    me = lax.axis_index("shot")
    row, column = iota(rows.shape, 0), iota(rows.shape, 1)
    way = row % WAYS
    target = jnp.where(
        way == 0,
        me ^ PARTNER[0],
        jnp.where(way == 1, me ^ PARTNER[1], jnp.where(way == 2, me ^ PARTNER[2], me ^ PARTNER[3])),
    )

    def along_lanes(values, offset):
        return jnp.sum(jnp.where(column == row + offset, values, 0.0), axis=0, keepdims=True)

    got = jnp.sum(jnp.where(column == base + me, rows, 0.0), axis=1, keepdims=True)
    sent = jnp.sum(jnp.where(column == base + target, rows, 0.0), axis=1, keepdims=True)
    lane = iota((1, LANES), 1)
    over = flag(least.reshape(1, 1) > STEPS + 0.5)
    table = along_lanes(got, 0) + along_lanes(sent, SEND_AT) + jnp.where(lane == FLAG_AT, over, 0.0)
    mine = [
        along_lanes(jnp.sum(jnp.where(column == me, count, 0.0), axis=1, keepdims=True), 0)
        for count in counts
    ]
    early = jnp.sum(
        jnp.where(lane == me, flag(second_early), 0.0), axis=1, keepdims=True
    ) + jnp.zeros((1, LANES), jnp.float32)
    blank = jnp.zeros((4, LANES), jnp.float32)
    out_ref[...] = jnp.concatenate([table, *mine, early, blank], axis=0).astype(jnp.int32)


def schedule(pairs):
    first, second = pairs[:, 0], pairs[:, 1]
    ends = jnp.stack([jnp.concatenate([first, second]), jnp.concatenate([second, first])])
    return pl.pallas_call(
        schedule_kernel,
        out_shape=jax.ShapeDtypeStruct((8, LANES), jnp.int32),
        in_specs=[VMEM],
        out_specs=VMEM,
        scratch_shapes=[pltpu.VMEM((GROUPS, 32, LANES), jnp.float32)],
        compiler_params=PARAMS,
        cost_estimate=pl.CostEstimate(
            flops=100_000_000, bytes_accessed=10_000_000, transcendentals=0
        ),
        name="schedule",
    )(ends)


def items_kernel(local_ref, first_ref, second_ref, value_buf, sems):
    out_refs = (first_ref, second_ref)
    keys = [
        pltpu.make_async_copy(local_ref.at[shot, 1], out_refs[shot].at[0], sems.at[shot])
        for shot in range(2)
    ]
    values = [
        pltpu.make_async_copy(local_ref.at[shot, 2], value_buf.at[shot], sems.at[2 + shot])
        for shot in range(2)
    ]
    for copy in values + keys:
        copy.start()
    for shot in range(2):
        values[shot].wait()
        out_refs[shot][1] = value_buf[shot].T
    for copy in keys:
        copy.wait()


def make_items(local):
    shots, _, tokens, width = local.shape
    return pl.pallas_call(
        items_kernel,
        out_shape=[jax.ShapeDtypeStruct((2, width, tokens), local.dtype)] * shots,
        in_specs=[ANY],
        out_specs=[VMEM] * shots,
        scratch_shapes=[
            pltpu.VMEM((shots, tokens, width), local.dtype),
            pltpu.SemaphoreType.DMA((4,)),
        ],
        compiler_params=PARAMS,
        name="items",
    )(local)


def queries_kernel(local_ref, query_ref, buf, sems):
    copies = [
        pltpu.make_async_copy(local_ref.at[shot, 0], buf.at[shot], sems.at[shot])
        for shot in range(2)
    ]
    for copy in copies:
        copy.start()
    for shot in range(2):
        copies[shot].wait()
        query_ref[shot] = buf[shot].T


def make_queries(local):
    shots, _, tokens, width = local.shape
    return pl.pallas_call(
        queries_kernel,
        out_shape=jax.ShapeDtypeStruct((shots, width, tokens), local.dtype),
        in_specs=[ANY],
        out_specs=VMEM,
        scratch_shapes=[
            pltpu.VMEM((shots, tokens, width), local.dtype),
            pltpu.SemaphoreType.DMA((shots,)),
        ],
        compiler_params=PARAMS,
        name="queries",
    )(local)


def attend_kernel(slots, first, which, ending, later, table_ref, query_ref, *refs):
    count = len(slots)
    item_refs, refs = refs[:count], refs[count:]
    if not first:
        old_acc_ref, old_stat_ref, *refs = refs
    refs = refs[later:]
    if ending:
        out_refs, refs = refs[:-2], refs[-2:]
    acc_ref, stat_ref = refs
    shots, width, tokens = query_ref.shape
    heads = width // HEAD_DIM
    early = table_ref[EARLY_ROW, 0]
    chosen = {"early": early, "late": 1 - early}.get(which)

    def times_of(slot, shot):
        kind, at = slots[slot]
        if kind == "own":
            return jnp.where(shot == at, 1, 0)
        item = table_ref[0, at]
        return jnp.where(item >= 0, table_ref[COUNT_ROW + shot, jnp.maximum(item, 0)], 0)

    if first:
        acc_ref[...] = jnp.zeros_like(acc_ref)
        stat_ref[:, :, 0:1, :] = jnp.full_like(stat_ref[:, :, 0:1, :], -1e30)
        stat_ref[:, :, 1:2, :] = jnp.zeros_like(stat_ref[:, :, 1:2, :])
    elif which != "both" and old_acc_ref.shape[0] > 1:
        acc_ref[0] = old_acc_ref[chosen]
        stat_ref[0] = old_stat_ref[chosen]
    else:
        acc_ref[...] = old_acc_ref[...]
        stat_ref[...] = old_stat_ref[...]

    def block(slot, shot, at, times):
        each = range(heads)
        spans = [pl.ds(head * HEAD_DIM, HEAD_DIM) for head in each]
        old = [acc_ref[at, head] for head in each]
        old_top = [stat_ref[at, head, 0:1, :] for head in each]
        old_sum = [stat_ref[at, head, 1:2, :] for head in each]
        weight = times.astype(jnp.float32)
        scores = [
            jnp.dot(
                item_refs[slot][0, :, span], query_ref[shot, span, :],
                preferred_element_type=jnp.float32,
            )
            for span in spans
        ]
        top = [
            jnp.maximum(a, jnp.max(score, axis=0, keepdims=True))
            for a, score in zip(old_top, scores)
        ]
        expo = [jnp.exp2(score * SCALE - a * SCALE) for score, a in zip(scores, top)]
        fade = [jnp.exp2((a - b) * SCALE) for a, b in zip(old_top, top)]
        part = [
            jnp.dot(
                item_refs[slot][1, span, :], e.astype(jnp.bfloat16),
                preferred_element_type=jnp.float32,
            )
            for span, e in zip(spans, expo)
        ]
        total = [jnp.sum(e, axis=0, keepdims=True) for e in expo]
        for head in each:
            acc_ref[at, head] = old[head] * fade[head] + part[head] * weight
            stat_ref[at, head, 0:1, :] = top[head]
            stat_ref[at, head, 1:2, :] = old_sum[head] * fade[head] + total[head] * weight

    for slot in range(count):
        for at in range(shots if which == "both" else 1):
            shot = at if which == "both" else chosen
            if slots[slot][0] == "own":
                if slots[slot][1] == shot:
                    block(slot, shot, at, jnp.int32(1))
                continue
            times = times_of(slot, shot)

            @pl.when(times > 0)
            def _():
                block(slot, shot, at, times)

    if ending:
        for head in range(heads):
            value = acc_ref[0, head] / stat_ref[0, head, 1:2, :]
            value = value.T.astype(jnp.bfloat16)
            size = tokens // len(out_refs)
            for piece, out_ref in enumerate(out_refs):
                out_ref[:, pl.ds(head * HEAD_DIM, HEAD_DIM)] = value[
                    piece * size : (piece + 1) * size
                ]


def attend(slots, table, query, items, state=None, which="both", pieces=0, after=()):
    shots, width, tokens = query.shape
    heads = width // HEAD_DIM
    kept = shots if which == "both" else 1
    acc = jax.ShapeDtypeStruct((kept, heads, HEAD_DIM, tokens), jnp.float32)
    stat = jax.ShapeDtypeStruct((kept, heads, 8, tokens), jnp.float32)
    count = len(slots)
    if pieces:
        out = [jax.ShapeDtypeStruct((tokens // pieces, width), jnp.bfloat16)] * pieces
        scratch = [pltpu.VMEM(acc.shape, acc.dtype), pltpu.VMEM(stat.shape, stat.dtype)]
    else:
        out, scratch = [acc, stat], []
    blocks = 2
    return pl.pallas_call(
        functools.partial(
            attend_kernel, slots, state is None, which, pieces > 0, len(after)
        ),
        out_shape=out,
        in_specs=[SMEM, VMEM]
        + [VMEM] * count
        + [VMEM] * (0 if state is None else 2)
        + [ANY] * len(after),
        out_specs=[VMEM] * len(out),
        scratch_shapes=scratch,
        compiler_params=PARAMS,
        cost_estimate=pl.CostEstimate(
            flops=blocks * heads * 4 * tokens * tokens * HEAD_DIM,
            bytes_accessed=count * 2 * width * tokens * 2 + 4 * acc.size * 2,
            transcendentals=blocks * heads * tokens * tokens,
        ),
        name="attend",
    )(table, query, *items, *(() if state is None else state), *after)


def pick_kernel(step, held, table_ref, *refs):
    item_refs, out_refs, sems = refs[:held], refs[-1 - WAYS : -1], refs[-1]
    shots = 2
    me = lax.axis_index("shot")

    def copy(slot, way):
        return pltpu.make_async_copy(item_refs[slot], out_refs[way], sems.at[way])

    wanted = [table_ref[0, SEND_AT + step * WAYS + way] for way in range(WAYS)]
    for slot in range(held):
        item = me * shots + slot if slot < shots else table_ref[0, slot - shots]
        for way in range(WAYS):
            @pl.when((wanted[way] >= 0) & (wanted[way] == item))
            def _():
                copy(slot, way).start()
    for way in range(WAYS):
        @pl.when(wanted[way] >= 0)
        def _():
            copy(0, way).wait()


def pick(step, table, items, after):
    one = jax.ShapeDtypeStruct(items[0].shape, items[0].dtype)
    return pl.pallas_call(
        functools.partial(pick_kernel, step, len(items)),
        out_shape=[one] * WAYS,
        in_specs=[SMEM] + [ANY] * (len(items) + len(after)),
        out_specs=[VMEM] * WAYS,
        scratch_shapes=[pltpu.SemaphoreType.DMA((WAYS,))],
        compiler_params=PARAMS,
        cost_estimate=pl.CostEstimate(
            flops=0, bytes_accessed=2 * WAYS * one.size * 2, transcendentals=0
        ),
        name="pick",
    )(table, *items, *after)


def cut_kernel(moves, wide, w_ref, *refs):
    out_refs, sems = refs[-1 - len(moves) : -1], refs[-1]
    index = lax.axis_index("head")
    copies = []
    for at, (even, odd) in enumerate(moves):
        chip = (index // 2) ^ jnp.where(index % 2 == 0, even, odd)
        start = pl.multiple_of(chip * wide, HEAD_DIM)
        copies.append(
            pltpu.make_async_copy(w_ref.at[:, pl.ds(start, wide)], out_refs[at], sems.at[at])
        )
    for copy in copies:
        copy.start()
    for copy in copies:
        copy.wait()


def cut_weights(w_out, moves, after):
    depth, wide = w_out.shape[0], 2 * (w_out.shape[1] // lax.axis_size("head"))
    one = jax.ShapeDtypeStruct((depth, wide), w_out.dtype)
    return pl.pallas_call(
        functools.partial(cut_kernel, moves, wide),
        out_shape=[one] * len(moves),
        in_specs=[ANY] * (1 + len(after)),
        out_specs=[VMEM] * len(moves),
        scratch_shapes=[pltpu.SemaphoreType.DMA((len(moves),))],
        compiler_params=PARAMS,
        cost_estimate=pl.CostEstimate(
            flops=0, bytes_accessed=4 * len(moves) * one.size, transcendentals=0
        ),
        name="cut",
    )(w_out, *after)


def along_z(array, move):
    size = lax.axis_size("head")
    return lax.ppermute(array, "head", [(i, i ^ (2 * move[i % 2])) for i in range(size)])


def mix_kernel(shape, carried, split, *refs):
    count = sum(shape)
    row_refs, weights, refs = refs[:count], refs[count : count + len(shape)], refs[count + len(shape) :]
    total = None
    if carried:
        total, refs = refs[0][...], refs[1:]
    at = 0
    for pieces, weight_ref in zip(shape, weights):
        rows = [ref[...] for ref in row_refs[at : at + pieces]]
        at += pieces
        rows = rows[0] if pieces == 1 else jnp.concatenate(rows, axis=0)
        term = jnp.dot(rows, weight_ref[...], preferred_element_type=jnp.float32)
        total = term if total is None else total + term
    if not split:
        refs[0][...] = total
        return
    keep_ref, give_ref = refs
    half = keep_ref.shape[1]
    first = lax.axis_index("head") % 2 == 0
    low, high = total[:, :half], total[:, half:]
    keep_ref[...] = jnp.where(first, low, high)
    give_ref[...] = jnp.where(first, high, low).astype(give_ref.dtype)


def mix(rows, weights, carry=None, split=True):
    size, wide = sum(piece.shape[0] for piece in rows[0]), weights[0].shape[1]
    if split:
        out = [
            jax.ShapeDtypeStruct((size, wide // 2), jnp.float32),
            jax.ShapeDtypeStruct((size, wide // 2), jnp.bfloat16),
        ]
    else:
        out = [jax.ShapeDtypeStruct((size, wide), jnp.float32)]
    more = [] if carry is None else [carry]
    shape = tuple(len(pieces) for pieces in rows)
    return pl.pallas_call(
        functools.partial(mix_kernel, shape, carry is not None, split),
        out_shape=out,
        in_specs=[VMEM] * (sum(shape) + len(rows) + len(more)),
        out_specs=[VMEM] * len(out),
        compiler_params=PARAMS,
        cost_estimate=pl.CostEstimate(
            flops=2 * len(rows) * size * weights[0].shape[0] * wide,
            bytes_accessed=4 * size * wide,
            transcendentals=0,
        ),
        name="mix",
    )(*(piece for pieces in rows for piece in pieces), *weights, *more)


def swap_cores(give):
    size = lax.axis_size("head")
    return lax.ppermute(give, "head", [(i, i ^ 1) for i in range(size)])


def finish_kernel(table_ref, keep_a, give_a, keep_b, give_b, out_ref):
    early = table_ref[EARLY_ROW, 0]
    out_ref[early] = (keep_a[...] + give_a[...].astype(jnp.float32)).astype(out_ref.dtype)
    out_ref[1 - early] = (keep_b[...] + give_b[...].astype(jnp.float32)).astype(out_ref.dtype)


def finish(table, early, late):
    tokens, part = early[0].shape
    return pl.pallas_call(
        finish_kernel,
        out_shape=jax.ShapeDtypeStruct((2, tokens, part), jnp.bfloat16),
        in_specs=[SMEM] + [VMEM] * 4,
        out_specs=VMEM,
        compiler_params=PARAMS,
        name="finish",
    )(table, *early, *late)


def halve_kernel(first_ref, second_ref, *refs):
    half = first_ref.shape[0] // 2
    refs[-2][...] = first_ref[:half]
    refs[-1][...] = second_ref[half:]


def halve(first, second, after):
    half = jax.ShapeDtypeStruct((first.shape[0] // 2, first.shape[1]), first.dtype)
    return pl.pallas_call(
        halve_kernel,
        out_shape=[half] * 2,
        in_specs=[VMEM] * 2 + [ANY] * len(after),
        out_specs=[VMEM] * 2,
        compiler_params=PARAMS,
        name="halve",
    )(first, second, *after)


def spread_whole(rows, after):
    there, back = along_z(rows, THERE), along_z(rows, BACK)
    upper, lower = halve(there, back, after)
    return [[rows], [there], [back], [along_z(upper, BACK), along_z(lower, THERE)]]


def spread_halves(one, two):
    one_there, two_back = along_z(one, THERE), along_z(two, BACK)
    two_there, one_back = along_z(two, THERE), along_z(one, BACK)
    return [
        [one, two],
        [one_there, two_there],
        [one_back, two_back],
        [along_z(one_there, BACK), along_z(two_back, THERE)],
    ]


def gather_all(projected, table, w_out):
    me, size = lax.axis_index("shot"), lax.axis_size("shot")
    shots = projected.shape[0]
    local = jnp.transpose(projected, (0, 2, 1, 3))
    query, items = make_queries(local), list(make_items(local))
    lane = jnp.arange(LANES, dtype=jnp.int32)
    both = [("table", 0), ("table", 1)]
    state = attend([("own", 0), ("own", 1)], table, query, items)

    def shift(hop, carry):
        items, state = carry
        items = [lax.ppermute(item, "shot", ring(size, 1)) for item in items]
        source = (me + size - 1 - hop) % size
        names = table.at[0].set(jnp.where(lane < shots, source * shots + lane, -1))
        return items, list(attend(both, names, query, items, state))

    items, state = lax.fori_loop(0, size - 1, shift, (items, list(state)))
    done = table.at[0].set(-1)
    early = attend([], done, query, [], state, "early", 1)[0]
    late = attend([], done, query, [], state, "late", 2)
    own, *parts = cut_weights(w_out, (STAY, THERE, BACK, ACROSS), [])
    weights = [own] + [
        along_z(part, move) for part, move in zip(parts, (THERE, BACK, ACROSS))
    ]
    sides = []
    for rows in (spread_whole(early, []), spread_halves(*late)):
        keep, give = mix(rows, weights)
        sides.append((keep, swap_cores(give)))
    return finish(table, *sides)


def body(projected, pairs, w_out):
    local = jnp.transpose(projected, (0, 2, 1, 3))
    held = list(make_items(local))
    table = schedule(pairs)
    query = make_queries(local)
    own, part = cut_weights(w_out, (STAY, THERE), [table])
    weights = [own, along_z(part, THERE)]
    flag = table[0, FLAG_AT]
    state, arrived = None, []
    for step in range(STEPS):
        if step == 0:
            outs = (held[0], held[0], held[1], held[1])
        else:
            after = [query, flag[None]] if state is None else [state[1]]
            outs = pick(step, table, held, after + weights[step - 1 : step] * (step > 1))
        got = [lax.ppermute(out, "shot", permutation(way)) for way, out in enumerate(outs)]
        slots = [("table", (step - 1) * WAYS + way) for way in range(WAYS)]
        if step == 1:
            state = attend(slots, table, query, arrived)
        elif 1 < step < EARLY_STEPS:
            own_slots = [("own", 0), ("own", 1)] * (step == EARLY_STEPS - 1)
            state = attend(own_slots + slots, table, query, held[: len(own_slots)] + arrived, state)
        elif step == EARLY_STEPS:
            early = attend(slots, table, query, arrived, state, "early", 1)[0]
            state = attend(slots, table, query, arrived, state, "late", after=[early])
        if step in (1, 2):
            move = (BACK, ACROSS)[step - 1]
            weights.append(along_z(cut_weights(w_out, (move,), [state[1]])[0], move))
        arrived = got
        held = held + got

    slots = [("table", (STEPS - 1) * WAYS + way) for way in range(WAYS)]
    late = attend(slots, table, query, arrived, state, "late", 1)[0]
    keep, give = mix(spread_whole(early, [late]), weights)
    early_side = (keep, swap_cores(give))
    late_rows = spread_whole(late, [])
    partial = mix(late_rows[:3], weights[:3], split=False)[0]
    keep, give = mix(late_rows[3:], weights[3:], partial)
    late_side = (keep, swap_cores(give))
    return lax.cond(
        flag > 0,
        lambda: gather_all(projected, table, w_out),
        lambda: finish(table, early_side, late_side),
    )


def solution(mesh):
    in_specs = (P("shot", None, None, "head"), P(), P("head", None))
    out_specs = P("shot", None, "head")
    return jax.shard_map(body, mesh=mesh, in_specs=in_specs, out_specs=out_specs, check_vma=False)
```
